128 devices in a mesh: row: 16 (over z, y_lo, core), col: 8 (over x, y_hi).
Axes of the slice: x: 4, y: 4 (y_hi: 2, y_lo: 2; y = y_hi * 2 + y_lo), z: 4, core: 2. Of those that a mesh axis runs over, the one named last changes fastest.
Arguments:
- atom_feats: bfloat16 [32768, 128], P(('row', 'col')), may hold values from -6 to 6
- atom_gain: float32 [128], replicated, may hold values from 0.1 to 1.9
- atom_project: bfloat16 [128, 384], replicated, may hold values from -2 to 2
- atom_merge: bfloat16 [128, 128], replicated, may hold values from -0.5 to 0.5
- atom_up: bfloat16 [128, 768], replicated, may hold values from -0.5 to 0.5
- token_counts: int32 [128, 16], P(('row', 'col')), may hold values from 1 to 24, 256 in all within a row
- token_single: bfloat16 [2048, 768], P(('row', 'col')), may hold values from -6 to 6
- token_gain: float32 [768], replicated, may hold values from 0.1 to 1.9
- token_project: bfloat16 [768, 2304], replicated, may hold values from -0.21875 to 0.21875
- token_merge: bfloat16 [768, 768], replicated, may hold values from -0.21875 to 0.21875
- pair_state: bfloat16 [2048, 2048, 128], P('row', 'col'), may hold values from -6 to 6
- pair_gain: float32 [128], replicated, may hold values from 0.1 to 1.9
- bias_weight: bfloat16 [128, 16], replicated, may hold values from -5 to 5
- atom_down: bfloat16 [768, 128], replicated, may hold values from -0.21875 to 0.21875
- position_weight: bfloat16 [3, 128], replicated, may hold values from -0.5 to 0.5
- position_cotangent: float32 [3, 32768], P(None, ('row', 'col')), may hold values from -6 to 6
Outputs:
- positions: float32 [3, 32768], P(None, ('row', 'col'))
- token_update: bfloat16 [2048, 768], P(('row', 'col'))
- pair_grad: bfloat16 [2048, 2048, 128], P('row', 'col')
The draws below stay inside these ranges and needn't reach their ends.
Inputs may be any that keep to these rules, and one draw needn't show every extreme that they name: `token_counts`: each row sums to 256, and each row holds the value 24.
All inputs are finite; a program needn't handle non-finite values.
Results may differ from the reference program's by a relative error of at most 0.013.
The reference program's roundings to bfloat16 on the way count: a program that leaves them out, or rounds other values in their place, can miss the bound.
Values may be sent and summed in bfloat16 or wider, within the bound.
No kernel may reach another device: no remote copies, remote signals or barrier semaphores. Data moves between devices by JAX's collectives and lax.ppermute only.
A program may use at most 128 MiB of HBM per device.

```python
import math
import jax
import jax.numpy as jnp
import numpy as np
from jax import lax

ATOM_WIDTH = 128
ATOM_HEADS = 4
TOKEN_WIDTH = 768
TOKEN_HEADS = 16
PAIR_WIDTH = 128
ATOM_DEV = 256
TOK_SEG = 16
MOST_ATOMS = 24
SEGMENTS = 128
ATOMS = 32768
TOKENS = 2048


def draw_atom_feats(key, part):
    key = jax.random.fold_in(key, 1)
    noise_key = jax.random.fold_in(key, 0)
    values = jax.random.normal(noise_key, (ATOMS, ATOM_WIDTH), jnp.float32)
    return jnp.clip(values, -6.0, 6.0).astype(jnp.bfloat16)


def draw_atom_project(key, part):
    key = jax.random.fold_in(key, 2)
    weights = jnp.clip(jax.random.normal(key, (ATOM_WIDTH, 3 * ATOM_WIDTH), jnp.float32), -6.0, 6.0) * ATOM_WIDTH ** (-0.5)
    return weights.astype(jnp.bfloat16)


def draw_pair_state(key, part):
    key = jax.random.fold_in(key, 3)
    noise_key = jax.random.fold_in(key, 0)
    values = jax.random.normal(noise_key, (TOKENS, TOKENS, PAIR_WIDTH), jnp.float32)
    return jnp.clip(values, -6.0, 6.0).astype(jnp.bfloat16)


def draw_bias_weight(key, part):
    key = jax.random.fold_in(key, 4)
    weights = jnp.clip(jax.random.normal(key, (PAIR_WIDTH, TOKEN_HEADS), jnp.float32), -6.0, 6.0) * PAIR_WIDTH ** (-0.5)
    return weights.astype(jnp.bfloat16)


def level_of(own_key, extent, cuts, low, high):
    factor_of, own = 1.0, jax.random.fold_in(own_key, 6)
    for dim, parts in cuts:
        steps = jnp.exp(jax.random.uniform(jax.random.fold_in(own, dim), (parts,), jnp.float32, low / len(cuts), high / len(cuts)))
        factor_of = factor_of * jnp.repeat(steps, extent[dim] // parts).reshape([-1 if axis == dim else 1 for axis in range(len(extent))])
    return factor_of


def profile(amount, total, bound, lean):
    weights = [(1 << 20) // math.isqrt(grade ** lean) + 1 for grade in range(2, amount + 1)]
    surplus, given = total - bound - (amount - 1), [1] * (amount - 1)
    while surplus > 0:
        free = [i for i in range(amount - 1) if given[i] < bound]
        whole, budget = sum([weights[i] for i in free]), surplus
        for i in free:
            addition = min(bound - given[i], max(1, budget * weights[i] // whole), surplus)
            given[i] = given[i] + addition
            surplus = surplus - addition
    return np.array([bound] + given)


def uneven_parts(own_key, amount, total, bound, lean):
    if amount == 2:
        one = jax.random.randint(own_key, (), max(1, total - bound), min(bound, total - 1) + 1)
        return jnp.stack([one, total - one])
    sizes = jnp.asarray(profile(amount, total, bound, lean), jnp.int32)
    pairs = (amount - 1) // 2
    giver, receiver = sizes[1:1 + 2 * pairs:2], sizes[2:2 + 2 * pairs:2]
    room = jnp.minimum(giver - 1, bound - receiver)
    moved = jax.random.randint(jax.random.fold_in(own_key, 1), (pairs,), 0, 1 << 20) % (room + 1)
    sizes = sizes.at[1:1 + 2 * pairs:2].set(giver - moved).at[2:2 + 2 * pairs:2].set(receiver + moved)
    return sizes[jax.random.permutation(jax.random.fold_in(own_key, 2), amount)]


def scatter_about(stream_key, extent, scale, bound, cuts=(), kind=jnp.bfloat16):
    result = scale * jax.random.normal(stream_key, extent, jnp.float32)
    if cuts:
        result = result * level_of(stream_key, extent, cuts, -0.22, 0.18)
    return jnp.clip(result, -bound, bound).astype(kind)


def setup_inputs(seed: int = 0) -> dict:
    seeds = jax.random.split(jax.random.key(seed), 17)
    atom_feats = draw_atom_feats(jax.random.fold_in(seeds[16], 71), 0)
    atom_gain = jnp.clip(1.0 + 0.18 * jax.random.normal(seeds[1], (ATOM_WIDTH,), jnp.float32), 0.1, 1.9)
    atom_project = draw_atom_project(jax.random.fold_in(seeds[16], 71), 0)
    atom_merge = scatter_about(seeds[3], (ATOM_WIDTH, ATOM_WIDTH), ATOM_WIDTH ** -0.5, 0.5)
    atom_up = scatter_about(seeds[4], (ATOM_WIDTH, TOKEN_WIDTH), ATOM_WIDTH ** -0.5, 0.5)
    token_counts = jax.vmap(lambda own: uneven_parts(own, TOK_SEG, ATOM_DEV, MOST_ATOMS, 2))(jax.random.split(seeds[5], SEGMENTS)).reshape((SEGMENTS, TOK_SEG)).astype(jnp.int32)
    token_single = scatter_about(seeds[6], (TOKENS, TOKEN_WIDTH), 1.0, 6.0, ((0, 128),))
    token_gain = jnp.clip(1.0 + 0.18 * jax.random.normal(seeds[7], (TOKEN_WIDTH,), jnp.float32), 0.1, 1.9)
    token_project = scatter_about(seeds[8], (TOKEN_WIDTH, 3 * TOKEN_WIDTH), TOKEN_WIDTH ** -0.5, 0.21875)
    token_merge = scatter_about(seeds[9], (TOKEN_WIDTH, TOKEN_WIDTH), TOKEN_WIDTH ** -0.5, 0.21875)
    pair_state = draw_pair_state(jax.random.fold_in(seeds[16], 71), 0)
    pair_gain = jnp.clip(1.0 + 0.18 * jax.random.normal(seeds[11], (PAIR_WIDTH,), jnp.float32), 0.1, 1.9)
    bias_weight = draw_bias_weight(jax.random.fold_in(seeds[16], 71), 0)
    atom_down = scatter_about(seeds[13], (TOKEN_WIDTH, ATOM_WIDTH), TOKEN_WIDTH ** -0.5, 0.21875)
    position_weight = scatter_about(seeds[14], (3, ATOM_WIDTH), ATOM_WIDTH ** -0.5, 0.5)
    position_cotangent = scatter_about(seeds[15], (3, ATOMS), 1.0, 6.0, ((1, 128),), jnp.float32)
    return dict(atom_feats=atom_feats, atom_gain=atom_gain, atom_project=atom_project, atom_merge=atom_merge, atom_up=atom_up, token_counts=token_counts, token_single=token_single, token_gain=token_gain, token_project=token_project, token_merge=token_merge, pair_state=pair_state, pair_gain=pair_gain, bias_weight=bias_weight, atom_down=atom_down, position_weight=position_weight, position_cotangent=position_cotangent)


EPS = 1e-05

def layer_norm(values, gain):
    center = values - lax.optimization_barrier(jnp.mean(values, axis=-1, keepdims=True))
    spread = lax.rsqrt(lax.optimization_barrier(jnp.mean(center * center, axis=-1, keepdims=True)) + EPS)
    standard = center * spread
    return (standard * gain, standard, spread)

def window_attend(queries, key_ext, value_ext, first_row, atom_total):
    blocks = queries.shape[0] // 32
    feature_width = queries.shape[1]
    head_size = feature_width // ATOM_HEADS

    def windows(extended):
        tile_rows = extended.reshape(blocks + 4, 32, feature_width)
        joined = jnp.concatenate([tile_rows[offset:offset + blocks] for offset in range(4)], axis=1)
        return joined.reshape(blocks, 128, ATOM_HEADS, head_size).astype(jnp.float32)
    query_heads = queries.reshape(blocks, 32, ATOM_HEADS, head_size).astype(jnp.float32)
    scores = jnp.einsum('bqhd,bkhd->bhqk', query_heads, windows(key_ext)) / math.sqrt(head_size)
    position = first_row - 48 + 32 * jnp.arange(blocks, dtype=jnp.int32)[:, None] + jnp.arange(128, dtype=jnp.int32)[None, :]
    inside = (position >= 0) & (position < atom_total)
    scores = jnp.where(inside[:, None, None, :], scores, -1e+30)
    row_max = lax.optimization_barrier(jnp.max(scores, axis=-1, keepdims=True))
    weights = jnp.exp(scores - row_max)
    row_total = lax.optimization_barrier(jnp.sum(weights, axis=-1))
    rounded = lax.optimization_barrier(weights.astype(jnp.bfloat16)).astype(jnp.float32)
    mixture = jnp.einsum('bhqk,bkhd->bqhd', rounded, windows(value_ext))
    mixture = mixture / jnp.transpose(row_total, (0, 2, 1))[:, :, :, None]
    return mixture.reshape(blocks * 32, feature_width).astype(jnp.bfloat16)

def reference(atom_feats, atom_gain, atom_project, atom_merge, atom_up, token_counts, token_single, token_gain, token_project, token_merge, pair_state, pair_gain, bias_weight, atom_down, position_weight, position_cotangent):
    atom_total = atom_feats.shape[0]
    feature_width = atom_feats.shape[1]
    normed = layer_norm(atom_feats.astype(jnp.float32), atom_gain)[0].astype(jnp.bfloat16)
    projected = jnp.dot(normed, atom_project, preferred_element_type=jnp.float32).astype(jnp.bfloat16)
    projected = lax.optimization_barrier(projected)
    queries = projected[:, :feature_width]
    key_ext = jnp.pad(projected[:, feature_width:2 * feature_width], ((48, 80), (0, 0)))
    value_ext = jnp.pad(projected[:, 2 * feature_width:], ((48, 80), (0, 0)))
    attended = window_attend(queries, key_ext, value_ext, 0, atom_total)
    hidden = (atom_feats.astype(jnp.float32) + jnp.dot(attended, atom_merge, preferred_element_type=jnp.float32)).astype(jnp.bfloat16)
    ends = jnp.cumsum(token_counts, axis=1).astype(jnp.int32)
    local_rows = jnp.arange(ATOM_DEV, dtype=jnp.int32)
    owner_local = lax.optimization_barrier(jnp.sum((local_rows[None, :, None] >= ends[:, None, :]).astype(jnp.int32), axis=2))
    owner = (owner_local + TOK_SEG * jnp.arange(token_counts.shape[0], dtype=jnp.int32)[:, None]).reshape(-1).astype(jnp.int32)
    lifted = jnp.maximum(jnp.dot(hidden, atom_up, preferred_element_type=jnp.float32), 0.0).astype(jnp.bfloat16)
    lifted = lax.optimization_barrier(lifted)
    sums = jax.ops.segment_sum(lifted.astype(jnp.float32), owner, num_segments=TOKENS)
    counts = token_counts.reshape(-1).astype(jnp.float32)
    token_state = sums / counts[:, None] + token_single.astype(jnp.float32)
    token_normed = layer_norm(token_state, token_gain)[0].astype(jnp.bfloat16)
    token_proj = jnp.dot(token_normed, token_project, preferred_element_type=jnp.float32).astype(jnp.bfloat16)
    token_proj = lax.optimization_barrier(token_proj)
    token_query = token_proj[:, :TOKEN_WIDTH]
    head_size = TOKEN_WIDTH // TOKEN_HEADS
    key_heads = token_proj[:, TOKEN_WIDTH:2 * TOKEN_WIDTH].reshape(TOKENS, TOKEN_HEADS, head_size).astype(jnp.float32)
    value_heads = token_proj[:, 2 * TOKEN_WIDTH:].reshape(TOKENS, TOKEN_HEADS, head_size).astype(jnp.float32)
    bias_matrix = bias_weight.astype(jnp.float32)
    block_rows = math.gcd(TOKENS, 128)
    count_blocks = TOKENS // block_rows

    def block_scores(start):
        tile = lax.dynamic_slice_in_dim(pair_state, start, block_rows, 0).astype(jnp.float32)
        normed_pair, standard, inv_spread = layer_norm(tile, pair_gain)
        rounded_pair = lax.optimization_barrier(normed_pair.astype(jnp.bfloat16)).astype(jnp.float32)
        bias = jnp.einsum('ijc,ch->hij', rounded_pair, bias_matrix, precision=lax.Precision.HIGHEST)
        query_heads = lax.dynamic_slice_in_dim(token_query, start, block_rows, 0).reshape(block_rows, TOKEN_HEADS, head_size).astype(jnp.float32)
        scores = jnp.einsum('ihd,jhd->hij', query_heads, key_heads, precision=lax.Precision.HIGHEST) / math.sqrt(head_size) + bias
        return (scores, standard, inv_spread)

    def forward_block(block):
        scores = block_scores(block * block_rows)[0]
        row_max = lax.optimization_barrier(jnp.max(scores, axis=-1))
        weights = jnp.exp(scores - row_max[:, :, None])
        row_total = lax.optimization_barrier(jnp.sum(weights, axis=-1))
        rounded = lax.optimization_barrier(weights.astype(jnp.bfloat16)).astype(jnp.float32)
        output = jnp.einsum('hij,jhd->ihd', rounded, value_heads, precision=lax.Precision.HIGHEST)
        return (output / jnp.transpose(row_total)[:, :, None], row_max, row_total)
    attention, score_max, score_total = lax.map(forward_block, jnp.arange(count_blocks, dtype=jnp.int32))
    flat_attention = attention.reshape(TOKENS, TOKEN_WIDTH)
    token_update = (token_state + jnp.dot(flat_attention.astype(jnp.bfloat16), token_merge, preferred_element_type=jnp.float32)).astype(jnp.bfloat16)
    lowered = lax.optimization_barrier(jnp.dot(token_update, atom_down, preferred_element_type=jnp.float32).astype(jnp.bfloat16))
    hidden_next = (hidden.astype(jnp.float32) + lowered[owner].astype(jnp.float32)).astype(jnp.bfloat16)
    positions = lax.dot_general(position_weight, hidden_next, (((1,), (1,)), ((), ())), preferred_element_type=jnp.float32)
    grad_hidden = jnp.dot(position_cotangent.T, position_weight.astype(jnp.float32), precision=lax.Precision.HIGHEST).astype(jnp.bfloat16)
    grad_hidden = lax.optimization_barrier(grad_hidden)
    grad_tokens = jax.ops.segment_sum(grad_hidden.astype(jnp.float32), owner, num_segments=TOKENS).astype(jnp.bfloat16)
    grad_update = lax.dot_general(grad_tokens, atom_down, (((1,), (1,)), ((), ())), preferred_element_type=jnp.float32).astype(jnp.bfloat16)
    grad_mix = lax.dot_general(grad_update, token_merge, (((1,), (1,)), ((), ())), preferred_element_type=jnp.float32).astype(jnp.bfloat16)
    grad_mix = lax.optimization_barrier(grad_mix)
    mix_heads = grad_mix.reshape(count_blocks, block_rows, TOKEN_HEADS, head_size)

    def backward_block(items):
        block, mix_part, out_part, max_part, total_part = items
        scores, standard, inv_spread = block_scores(block * block_rows)
        probs = jnp.exp(scores - max_part[:, :, None]) / total_part[:, :, None]
        mix_float = mix_part.astype(jnp.float32)
        grad_probs = jnp.einsum('ihd,jhd->hij', mix_float, value_heads, precision=lax.Precision.HIGHEST)
        inner = jnp.einsum('ihd,ihd->hi', mix_float, out_part, precision=lax.Precision.HIGHEST)
        grad_scores = probs * (grad_probs - inner[:, :, None])
        grad_normed = jnp.einsum('hij,ch->ijc', grad_scores, bias_matrix, precision=lax.Precision.HIGHEST)
        scaled = grad_normed * pair_gain
        first_mean = lax.optimization_barrier(jnp.mean(scaled, axis=-1, keepdims=True))
        second_mean = lax.optimization_barrier(jnp.mean(scaled * standard, axis=-1, keepdims=True))
        return (inv_spread * (scaled - first_mean - standard * second_mean)).astype(jnp.bfloat16)
    pair_grad = lax.map(backward_block, (jnp.arange(count_blocks, dtype=jnp.int32), mix_heads, attention, score_max, score_total))
    return (positions, token_update, pair_grad.reshape(TOKENS, TOKENS, PAIR_WIDTH))
```

```python
import math

import jax
import jax.numpy as jnp
from jax import lax
from jax.experimental import pallas as pl
from jax.experimental.pallas import tpu as pltpu
from jax.sharding import PartitionSpec as P

ATOM_HEADS = 4
EPS = 1e-05
NEGATIVE = -1e30
LEFT, RIGHT = 48, 80
WINDOW = 32
KEYS = 128
LANES = 128
GROUP = 8
F32 = jnp.float32
BF16 = jnp.bfloat16
NT = (((1,), (1,)), ((), ()))
TN = (((0,), (0,)), ((), ()))
MIB = 1 << 20


def iota(shape, axis):
    return lax.broadcasted_iota(jnp.int32, shape, axis)


def dot(a, b):
    return jnp.dot(a, b, preferred_element_type=F32)


def dot_nt(a, b):
    return lax.dot_general(a, b, NT, preferred_element_type=F32)


def dot_tn(a, b):
    return lax.dot_general(a, b, TN, preferred_element_type=F32)


def split(value):
    high = value.astype(BF16)
    return high, (value - high.astype(F32)).astype(BF16)


def normalize(values, gain):
    center = values - jnp.mean(values, axis=-1, keepdims=True)
    spread = lax.rsqrt(jnp.mean(center * center, axis=-1, keepdims=True) + EPS)
    return center * spread * gain


def head_mask(rows, width, heads):
    size = width // heads
    head = iota((rows, width), 0) % heads
    column = iota((rows, width), 1)
    return ((column >= head * size) & (column < (head + 1) * size)).astype(F32)


def pair_kernel(x_ref, gain_ref, weight_ref, *rest):
    bias_ref, spread_ref, standard_ref, block_ref, ones_ref = rest[-5:]
    heads = weight_ref.shape[1]
    width = x_ref.shape[2]

    @pl.when(pl.program_id(0) == 0)
    def _():
        lane = iota((heads, LANES), 1)
        repeat = (lane % heads == iota((heads, LANES), 0)).astype(BF16)
        tiled = dot(weight_ref[...], repeat)
        owner = iota((width, LANES), 1) // heads
        for i in range(GROUP):
            block_ref[i * width : (i + 1) * width, :] = jnp.where(owner == i, tiled, 0.0).astype(BF16)
        same = (iota((2 * width, 2 * width), 0) // width) == (iota((2 * width, 2 * width), 1) // width)
        ones_ref[...] = jnp.where(same, 1.0 / width, 0.0).astype(BF16)

    gain = jnp.concatenate([gain_ref[...], gain_ref[...]], axis=1)
    ones = ones_ref[...]
    keys = x_ref.shape[1]
    owner = iota((keys, LANES), 1) // heads
    bias = jnp.zeros((keys, LANES), F32)
    spread_all = jnp.zeros((keys, LANES), F32)
    for i in range(0, GROUP, 2):
        x = jnp.concatenate([x_ref[i], x_ref[i + 1]], axis=1)
        center = x.astype(F32) - dot(x, ones)
        high, low = split(center * center)
        spread = lax.rsqrt(dot(high, ones) + dot(low, ones) + EPS)
        standard = center * spread
        rounded = standard.astype(BF16)
        standard_ref[i] = rounded[:, :width]
        standard_ref[i + 1] = rounded[:, width:]
        normed = (standard * gain).astype(BF16)
        bias = bias + dot(normed, block_ref[i * width : (i + 2) * width, :])
        spread_all = jnp.where(owner == i, spread[:, :width], spread_all)
        spread_all = jnp.where(owner == i + 1, spread[:, width:], spread_all)
    bias_ref[...] = bias
    spread_ref[...] = spread_all


def pair_forward(pair, gain, weight, first, count, previous=None):
    rows, keys, width = pair.shape
    heads = weight.shape[1]
    lanes = rows * heads
    outs = (
        jax.ShapeDtypeStruct((keys, lanes), F32),
        jax.ShapeDtypeStruct((keys, lanes), F32),
        jax.ShapeDtypeStruct(pair.shape, BF16),
    )
    before = () if previous is None else tuple(previous)
    return pl.pallas_call(
        pair_kernel,
        grid=(count,),
        in_specs=[
            pl.BlockSpec((GROUP, keys, width), lambda g: (g + first, 0, 0)),
            pl.BlockSpec((1, width), lambda g: (0, 0)),
            pl.BlockSpec((width, heads), lambda g: (0, 0)),
        ]
        + [pl.BlockSpec(memory_space=pl.ANY)] * len(before),
        out_specs=(
            pl.BlockSpec((keys, LANES), lambda g: (0, g + first)),
            pl.BlockSpec((keys, LANES), lambda g: (0, g + first)),
            pl.BlockSpec((GROUP, keys, width), lambda g: (g + first, 0, 0)),
        ),
        out_shape=outs,
        scratch_shapes=[
            pltpu.VMEM((GROUP * width, LANES), BF16),
            pltpu.VMEM((2 * width, 2 * width), BF16),
        ],
        input_output_aliases={3 + i: i for i in range(len(before))},
        compiler_params=pltpu.CompilerParams(vmem_limit_bytes=24 * MIB),
        cost_estimate=pl.CostEstimate(
            flops=count * GROUP * keys * width * 800, bytes_accessed=count * GROUP * keys * width * 5, transcendentals=0
        ),
        name="pair_forward",
    )(pair, gain, weight, *before)


def atom_kernel(
    first_ref, left_ref, own_ref, right_ref, gain_ref, project_ref, merge_ref, up_ref,
    counts_ref, single_ref, token_gain_ref, weight_ref, cotangent_ref,
    hidden_ref, state_ref, send_ref, key_ref, value_ref, query_ref, attended_ref,
):
    atoms, width = own_ref.shape
    tokens = single_ref.shape[0]
    first = first_ref[0]
    feats = jnp.concatenate(
        [left_ref[atoms - LEFT :, :], own_ref[...], right_ref[:RIGHT, :]], axis=0
    )
    normed = normalize(feats.astype(F32), gain_ref[...]).astype(BF16)
    projected = dot(normed, project_ref[...]).astype(BF16)
    query_ref[...] = projected[LEFT : LEFT + atoms, :width]
    key_ref[...] = projected[:, width : 2 * width]
    value_ref[...] = projected[:, 2 * width :]
    size = width // ATOM_HEADS
    rows = ATOM_HEADS * WINDOW
    lane_head = iota((rows, width), 1) // size
    row_head = iota((rows, width), 0) // WINDOW
    mask = lane_head == row_head
    key_index = iota((rows, KEYS), 1)
    total = jnp.int32(atoms) * first_ref[1]
    for b in range(atoms // WINDOW):
        at = b * WINDOW
        queries = jnp.concatenate([query_ref[at : at + WINDOW, :]] * ATOM_HEADS, axis=0)
        queries = jnp.where(mask, queries.astype(F32), 0.0).astype(BF16)
        scores = dot_nt(queries, key_ref[at : at + KEYS, :]) / math.sqrt(size)
        position = first - LEFT + at + key_index
        scores = jnp.where((position >= 0) & (position < total), scores, NEGATIVE)
        weights = jnp.exp(scores - jnp.max(scores, axis=1, keepdims=True))
        row_total = jnp.sum(weights, axis=1, keepdims=True)
        mixture = dot(weights.astype(BF16), value_ref[at : at + KEYS, :]) / row_total
        mixture = jnp.where(mask, mixture, 0.0)
        joined = mixture[:WINDOW]
        for h in range(1, ATOM_HEADS):
            joined = joined + mixture[h * WINDOW : (h + 1) * WINDOW]
        attended_ref[at : at + WINDOW, :] = joined.astype(BF16)
    hidden = (own_ref[...].astype(F32) + dot(attended_ref[...], merge_ref[...])).astype(BF16)
    hidden_ref[...] = hidden
    lifted = jnp.maximum(dot(hidden, up_ref[...]), 0.0).astype(BF16)
    counts_row = counts_ref[...].astype(F32)
    square = jnp.broadcast_to(counts_row, (tokens, tokens))
    above = iota((tokens, tokens), 0)
    below = iota((tokens, tokens), 1)
    counts_col = jnp.sum(jnp.where(above == below, square, 0.0), axis=1, keepdims=True)
    ends = jnp.sum(jnp.where(below <= above, square, 0.0), axis=1, keepdims=True)
    atom = iota((tokens, atoms), 1).astype(F32)
    member = ((atom < ends) & (atom >= ends - counts_col)).astype(F32).astype(BF16)
    state = dot(member, lifted) / counts_col + single_ref[...].astype(F32)
    state_ref[...] = state
    token_normed = normalize(state, token_gain_ref[...]).astype(BF16)
    turned = jnp.transpose(
        jnp.concatenate([cotangent_ref[...], jnp.zeros((LANES - 3, atoms), F32)], axis=0)
    )
    position_weight = weight_ref[...].astype(F32)
    grad_hidden = turned[:, 0:1] * position_weight[0:1, :]
    for k in range(1, 3):
        grad_hidden = grad_hidden + turned[:, k : k + 1] * position_weight[k : k + 1, :]
    grad_tokens = dot(member, grad_hidden.astype(BF16)).astype(BF16)
    packed = jnp.concatenate([token_normed, grad_tokens], axis=1)
    for c in range(send_ref.shape[0]):
        send_ref[c] = packed


def whole(array):
    zeros = (0,) * array.ndim
    return pl.BlockSpec(array.shape, lambda *_: zeros)


def atom_stage(first, left, own, right, gain, project, merge, up, counts, single, token_gain, weight, cotangent, copies):
    atoms, width = own.shape
    tokens, token_width = single.shape
    arrays = (left, own, right, gain, project, merge, up, counts, single, token_gain, weight, cotangent)
    outs = (
        jax.ShapeDtypeStruct((atoms, width), BF16),
        jax.ShapeDtypeStruct((tokens, token_width), F32),
        jax.ShapeDtypeStruct((copies, tokens, token_width + width), BF16),
    )
    return pl.pallas_call(
        atom_kernel,
        grid=(1,),
        in_specs=[pl.BlockSpec(memory_space=pltpu.SMEM)] + [whole(a) for a in arrays],
        out_specs=tuple(whole(a) for a in outs),
        out_shape=outs,
        scratch_shapes=[
            pltpu.VMEM((LEFT + atoms + RIGHT, width), BF16),
            pltpu.VMEM((LEFT + atoms + RIGHT, width), BF16),
            pltpu.VMEM((atoms, width), BF16),
            pltpu.VMEM((atoms, width), BF16),
        ],
        compiler_params=pltpu.CompilerParams(vmem_limit_bytes=16 * MIB),
        cost_estimate=pl.CostEstimate(flops=400 * MIB, bytes_accessed=2 * MIB, transcendentals=0),
        name="atom_stage",
    )(first, *arrays)


def query_kernel(rows_ref, project_ref, down_ref, merge_ref, query_ref, mix_ref):
    width = project_ref.shape[0]
    rows = rows_ref[...]
    query_ref[...] = dot(rows[:, :width], project_ref[...]).astype(BF16)
    update = dot_nt(rows[:, width:], down_ref[...]).astype(BF16)
    mix_ref[...] = dot_nt(update, merge_ref[...]).astype(BF16)


def query_stage(rows, project, down, merge):
    count = rows.shape[0]
    width = project.shape[0]
    out = jax.ShapeDtypeStruct((count, width), BF16)
    return pl.pallas_call(
        query_kernel,
        grid=(1,),
        in_specs=[whole(rows), pl.BlockSpec((width, width), lambda g: (0, 0)), whole(down), whole(merge)],
        out_specs=(whole(out), whole(out)),
        out_shape=(out, out),
        compiler_params=pltpu.CompilerParams(vmem_limit_bytes=16 * MIB),
        cost_estimate=pl.CostEstimate(flops=400 * MIB, bytes_accessed=4 * MIB, transcendentals=0),
        name="query_stage",
    )(rows, project, down, merge)


def attend_kernel(
    half_ref, first_ref, second_ref, key_project_ref, value_project_ref, query_ref, mix_ref,
    bias_ref, spread_ref,
    weight_ref, grad_ref, small_ref, send_ref, key_ref, value_ref,
):
    step = pl.program_id(0)
    width = key_project_ref.shape[0]
    heads = 16
    stat_rows = 2 * 8

    @pl.when(step == 0)
    def _():
        count = first_ref.shape[0]
        swap = half_ref[0] == 1
        first = first_ref[:, :width]
        second = second_ref[:, :width]
        low = jnp.where(swap, second, first)
        high = jnp.where(swap, first, second)
        for at, rows in ((0, low), (count, high)):
            key_ref[at : at + count, :] = dot(rows, key_project_ref[...]).astype(BF16)
            value_ref[at : at + count, :] = dot(rows, value_project_ref[...]).astype(BF16)

    mask = head_mask(heads, width, heads)
    rows = query_ref.shape[0]

    def expanded(ref):
        spread_out = ref[...].astype(F32)[:, None, :] * mask[None]
        return spread_out.reshape(rows * heads, width).astype(BF16)

    keys = key_ref[...]
    values = value_ref[...]
    scores = dot_nt(keys, expanded(query_ref)) / math.sqrt(width // heads) + bias_ref[...]
    grad_probs = dot_nt(values, expanded(mix_ref))
    row_max = jnp.max(scores, axis=0, keepdims=True)
    weights = jnp.exp(scores - row_max)
    row_total = jnp.sum(weights, axis=0, keepdims=True)
    rounded = weights.astype(BF16)
    inner = jnp.sum(rounded.astype(F32) * grad_probs, axis=0, keepdims=True)
    weight_ref[...] = weights * spread_ref[...]
    grad_ref[...] = grad_probs
    small_ref[...] = (bias_ref[...] * (1.0 / LANES)).astype(BF16)
    per = rows * heads // LANES
    for k, stat in enumerate((row_max, row_total, inner)):
        for p in range(per):
            send_ref[0, pl.ds(k * stat_rows + step * per + p, 1), :] = stat[:, p * LANES : (p + 1) * LANES]
    mixture = dot_tn(rounded, values).reshape(rows, heads, width) * mask[None]
    part = jnp.sum(mixture, axis=1)
    for t in range(width // LANES):
        at = 3 * stat_rows + t * rows
        send_ref[step, at : at + rows, :] = part[:, t * LANES : (t + 1) * LANES]

    @pl.when(step == pl.num_programs(0) - 1)
    def _():
        stats = send_ref[0, : 3 * stat_rows, :]
        for c in range(1, send_ref.shape[0]):
            send_ref[c, : 3 * stat_rows, :] = stats


def attend_stage(half, first, second, project, query, mix, bias, spread, owners):
    keys, lanes = bias.shape
    count, width = query.shape
    rows = count // owners
    chunk = lanes // owners
    stat_rows = 3 * lanes // LANES
    payload = jax.ShapeDtypeStruct((owners, stat_rows + rows * width // LANES, LANES), F32)
    tile = pl.BlockSpec((keys, chunk), lambda g: (0, g))
    return pl.pallas_call(
        attend_kernel,
        grid=(owners,),
        in_specs=[
            pl.BlockSpec(memory_space=pltpu.SMEM),
            whole(first),
            whole(second),
            pl.BlockSpec((width, width), lambda g: (0, 1)),
            pl.BlockSpec((width, width), lambda g: (0, 2)),
            pl.BlockSpec((rows, width), lambda g: (g, 0)),
            pl.BlockSpec((rows, width), lambda g: (g, 0)),
            tile,
            tile,
        ],
        out_specs=(tile, tile, tile, whole(payload)),
        out_shape=(
            jax.ShapeDtypeStruct((keys, lanes), F32),
            jax.ShapeDtypeStruct((keys, lanes), F32),
            jax.ShapeDtypeStruct((keys, lanes), BF16),
            payload,
        ),
        scratch_shapes=[pltpu.VMEM((keys, width), BF16), pltpu.VMEM((keys, width), BF16)],
        compiler_params=pltpu.CompilerParams(vmem_limit_bytes=32 * MIB),
        cost_estimate=pl.CostEstimate(flops=3000 * MIB, bytes_accessed=12 * MIB, transcendentals=0),
        name="attend_stage",
    )(half, first, second, project, project, query, mix, bias, spread)


def gradient_kernel(
    weight_ref, grad_ref, small_ref, standard_ref, received_ref, own_ref, gain_ref, bias_weight_ref,
    out_ref, block_ref, ones_ref, factor_ref, inner_ref,
):
    step = pl.program_id(0)
    width, heads = bias_weight_ref.shape
    rows = factor_ref.shape[0]

    @pl.when(step == 0)
    def _():
        lane = iota((heads, LANES), 1)
        repeat = (lane % heads == iota((heads, LANES), 0)).astype(BF16)
        tiled = jnp.transpose(dot(bias_weight_ref[...], repeat)) * gain_ref[...]
        tiled = tiled - jnp.mean(tiled, axis=1, keepdims=True)
        high, low = split(tiled)
        owner = iota((LANES, width), 0) // heads
        for i in range(GROUP):
            mine = owner == i
            at = slice(i * width, (i + 1) * width)
            block_ref[:LANES, at] = jnp.where(mine, high.astype(F32), 0.0).astype(BF16)
            block_ref[LANES:, at] = jnp.where(mine, low.astype(F32), 0.0).astype(BF16)
            ones = jnp.where(mine, 1.0, 0.0).astype(BF16)
            ones_ref[:LANES, at] = ones
            ones_ref[LANES:, at] = ones
        parts = received_ref.shape[0]
        top = received_ref[0, :rows, :]
        for s in range(1, parts):
            top = jnp.maximum(top, received_ref[s, :rows, :])
        total = jnp.zeros_like(top)
        inner = jnp.zeros_like(top)
        for s in range(parts):
            scale = jnp.exp(received_ref[s, :rows, :] - top)
            total = total + scale * received_ref[s, rows : 2 * rows, :]
            inner = inner + scale * received_ref[s, 2 * rows : 3 * rows, :]
        factor_ref[...] = jnp.exp(own_ref[0, :rows, :] - top) / total
        inner_ref[...] = inner / total

    factor = factor_ref[pl.ds(step, 1), :]
    inner = inner_ref[pl.ds(step, 1), :]
    grad = weight_ref[...] * factor * (grad_ref[...] - inner)
    rounded = grad.astype(BF16)
    left = jnp.concatenate([rounded, rounded], axis=1)
    high, low = split(grad * small_ref[...].astype(F32))
    right = jnp.concatenate([high, low], axis=1)
    for i in range(0, GROUP, 2):
        at = slice(i * width, (i + 2) * width)
        direct = dot(left, block_ref[:, at])
        along = dot(right, ones_ref[:, at])
        for k in range(2):
            part = slice(k * width, (k + 1) * width)
            out_ref[i + k] = (direct[:, part] - standard_ref[i + k].astype(F32) * along[:, part]).astype(BF16)


def gradient_stage(weights, grad, small, standard, received, own, gain, bias_weight):
    rows, keys, width = standard.shape
    tile = pl.BlockSpec((keys, LANES), lambda g: (0, g))
    block = pl.BlockSpec((GROUP, keys, width), lambda g: (g, 0, 0))
    return pl.pallas_call(
        gradient_kernel,
        grid=(rows // GROUP,),
        in_specs=[tile, tile, tile, block, whole(received), whole(own), whole(gain), whole(bias_weight)],
        out_specs=block,
        out_shape=jax.ShapeDtypeStruct(standard.shape, BF16),
        scratch_shapes=[
            pltpu.VMEM((2 * LANES, GROUP * width), BF16),
            pltpu.VMEM((2 * LANES, GROUP * width), BF16),
            pltpu.VMEM((rows // GROUP, LANES), F32),
            pltpu.VMEM((rows // GROUP, LANES), F32),
        ],
        compiler_params=pltpu.CompilerParams(vmem_limit_bytes=24 * MIB),
        cost_estimate=pl.CostEstimate(flops=16000 * MIB, bytes_accessed=22 * MIB, transcendentals=0),
        name="gradient_stage",
    )(weights, grad, small, standard, received, own, gain, bias_weight)


def update_kernel(
    column_ref, received_ref, state_ref, hidden_ref, counts_ref, merge_ref, down_ref, weight_ref,
    positions_ref, update_ref,
):
    column = column_ref[0]
    tokens, width = state_ref.shape
    heads = 16
    parts = received_ref.shape[0]
    stat_rows = (received_ref.shape[1] - tokens * width // LANES) // 3
    halves = tokens // GROUP

    def stats(kind, part):
        at = kind * stat_rows + column * halves
        return [received_ref[part, pl.ds(at + p, 1), :] for p in range(halves)]

    maxima = [stats(0, s) for s in range(parts)]
    totals = [stats(1, s) for s in range(parts)]
    sub = iota((tokens, LANES), 0)
    lane = iota((tokens, LANES), 1)
    scales = [[] for _ in range(parts)]
    for p in range(halves):
        top = maxima[0][p]
        for s in range(1, parts):
            top = jnp.maximum(top, maxima[s][p])
        exps = [jnp.exp(maxima[s][p] - top) for s in range(parts)]
        total = exps[0] * totals[0][p]
        for s in range(1, parts):
            total = total + exps[s] * totals[s][p]
        for s in range(parts):
            scales[s].append(exps[s] / total)
    mine = lane // heads == sub % GROUP
    rows = []
    for s in range(parts):
        picked = jnp.zeros((tokens, LANES), F32)
        for p in range(halves):
            picked = jnp.where(sub // GROUP == p, jnp.broadcast_to(scales[s][p], (tokens, LANES)), picked)
        rows.append(jnp.where(mine, picked, 0.0))
    stacked = jnp.concatenate(rows, axis=0)
    spread_out = head_mask(LANES, width, heads).astype(BF16)
    high, low = split(stacked)
    rest = stacked - high.astype(F32) - low.astype(F32)
    scale = dot(high, spread_out) + dot(low, spread_out) + dot(rest.astype(BF16), spread_out)
    pieces = []
    for t in range(width // LANES):
        at = 3 * stat_rows + t * tokens
        piece = jnp.zeros((tokens, LANES), F32)
        for s in range(parts):
            factor = scale[s * tokens : (s + 1) * tokens, t * LANES : (t + 1) * LANES]
            piece = piece + factor * received_ref[s, at : at + tokens, :]
        pieces.append(piece.astype(BF16))
    attention = jnp.concatenate(pieces, axis=1)
    update = (state_ref[...] + dot(attention, merge_ref[...])).astype(BF16)
    update_ref[...] = update
    lowered = dot(update, down_ref[...]).astype(BF16)
    atoms = hidden_ref.shape[0]
    counts_row = counts_ref[...].astype(F32)
    square = jnp.broadcast_to(counts_row, (tokens, tokens))
    above = iota((tokens, tokens), 0)
    below = iota((tokens, tokens), 1)
    counts_col = jnp.sum(jnp.where(above == below, square, 0.0), axis=1, keepdims=True)
    ends = jnp.sum(jnp.where(below <= above, square, 0.0), axis=1, keepdims=True)
    atom = iota((tokens, atoms), 1).astype(F32)
    member = ((atom < ends) & (atom >= ends - counts_col)).astype(F32).astype(BF16)
    hidden_next = (hidden_ref[...].astype(F32) + dot_tn(member, lowered)).astype(BF16)
    positions_ref[...] = dot_nt(weight_ref[...], hidden_next)


def update_stage(column, received, state, hidden, counts, merge, down, weight):
    tokens, width = state.shape
    arrays = (received, state, hidden, counts, merge, down, weight)
    outs = (
        jax.ShapeDtypeStruct((weight.shape[0], hidden.shape[0]), F32),
        jax.ShapeDtypeStruct((tokens, width), BF16),
    )
    return pl.pallas_call(
        update_kernel,
        grid=(1,),
        in_specs=[pl.BlockSpec(memory_space=pltpu.SMEM)] + [whole(a) for a in arrays],
        out_specs=tuple(whole(a) for a in outs),
        out_shape=outs,
        compiler_params=pltpu.CompilerParams(vmem_limit_bytes=16 * MIB),
        cost_estimate=pl.CostEstimate(flops=100 * MIB, bytes_accessed=3 * MIB, transcendentals=0),
        name="update_stage",
    )(column, *arrays)


def per_device(
    atom_feats, atom_gain, atom_project, atom_merge, atom_up, token_counts, token_single, token_gain,
    token_project, token_merge, pair_state, pair_gain, bias_weight, atom_down, position_weight,
    position_cotangent,
):
    both = ("row", "col")
    rows, columns = lax.axis_size("row"), lax.axis_size("col")
    devices = rows * columns
    row, column = lax.axis_index("row"), lax.axis_index("col")
    device = row * columns + column
    atoms = atom_feats.shape[0]
    left = lax.ppermute(atom_feats, both, [(i, i + 1) for i in range(devices - 1)])
    right = lax.ppermute(atom_feats, both, [(i + 1, i) for i in range(devices - 1)])
    gain = pair_gain.reshape(1, -1)
    groups = pair_state.shape[0] // GROUP
    cut = groups // 2
    pair_first = pair_forward(pair_state, gain, bias_weight, 0, cut)
    first_atom = jnp.stack([device * atoms, devices]).astype(jnp.int32)
    hidden, state, send = atom_stage(
        first_atom, left, atom_feats, right, atom_gain.reshape(1, -1), atom_project, atom_merge, atom_up,
        token_counts, token_single, token_gain.reshape(1, -1), position_weight, position_cotangent, columns,
    )
    gathered = lax.all_to_all(send, "col", 0, 0)
    gathered = gathered.reshape(-1, gathered.shape[-1])
    per_column = rows // columns
    routes = []
    for shift in range(per_column):
        route = []
        for c in range(columns):
            for k in range(per_column):
                for m in range(columns):
                    target = m + columns * ((k + shift) % per_column)
                    route.append(((per_column * c + k) * columns + m, target * columns + c))
        routes.append(route)
    first, second = [lax.ppermute(gathered, both, route) for route in routes]
    query, mix = query_stage(gathered, token_project, atom_down, token_merge)
    bias, spread, standard = pair_forward(pair_state, gain, bias_weight, cut, groups - cut, pair_first)
    half = (row // columns).astype(jnp.int32).reshape(1)
    weights, grad, small, payload = attend_stage(
        half, first, second, token_project, query, mix, bias, spread, columns
    )
    received = lax.all_to_all(payload, "col", 0, 0)
    positions, token_update = update_stage(
        column.astype(jnp.int32).reshape(1), received, state, hidden, token_counts, token_merge, atom_down,
        position_weight,
    )
    pair_grad = gradient_stage(weights, grad, small, standard, received, payload, gain, bias_weight)
    return (positions, token_update, pair_grad)


def solution(mesh):
    placed = (
        P(("row", "col"), None), P(), P(), P(), P(), P(("row", "col"), None), P(("row", "col"), None), P(),
        P(), P(), P("row", "col", None), P(), P(), P(), P(), P(None, ("row", "col")),
    )
    return jax.shard_map(
        per_device,
        mesh=mesh,
        in_specs=placed,
        out_specs=(P(None, ("row", "col")), P(("row", "col"), None), P("row", "col", None)),
        check_vma=False,
    )
```

```python
import math

import jax
import jax.numpy as jnp
from jax import lax
from jax.experimental import pallas as pl
from jax.experimental.pallas import tpu as pltpu
from jax.sharding import PartitionSpec as P

ATOM_HEADS = 4
EPS = 1e-05
NEGATIVE = -1e30
LEFT, RIGHT = 48, 80
WINDOW = 32
KEYS = 128
LANES = 128
GROUP = 8
STACK = 4
F32 = jnp.float32
BF16 = jnp.bfloat16
NT = (((1,), (1,)), ((), ()))
TN = (((0,), (0,)), ((), ()))
MIB = 1 << 20


def iota(shape, axis):
    return lax.broadcasted_iota(jnp.int32, shape, axis)


def dot(a, b):
    return jnp.dot(a, b, preferred_element_type=F32)


def dot_nt(a, b):
    return lax.dot_general(a, b, NT, preferred_element_type=F32)


def dot_tn(a, b):
    return lax.dot_general(a, b, TN, preferred_element_type=F32)


def split(value):
    high = value.astype(BF16)
    return high, (value - high.astype(F32)).astype(BF16)


def normalize(values, gain):
    center = values - jnp.mean(values, axis=-1, keepdims=True)
    spread = lax.rsqrt(jnp.mean(center * center, axis=-1, keepdims=True) + EPS)
    return center * spread * gain


def head_mask(rows, width, heads):
    size = width // heads
    head = iota((rows, width), 0) % heads
    column = iota((rows, width), 1)
    return ((column >= head * size) & (column < (head + 1) * size)).astype(F32)


def pair_kernel(x_ref, gain_ref, weight_ref, *rest):
    bias_ref, spread_ref, standard_ref, block_ref, ones_ref, normed_ref = rest[-6:]
    heads = weight_ref.shape[0]
    width = x_ref.shape[2]

    @pl.when(pl.program_id(0) == 0)
    def _():
        lane = iota((heads, LANES), 1)
        repeat = (lane % heads == iota((heads, LANES), 0)).astype(BF16)
        tiled = dot_tn(weight_ref[...], repeat)
        owner = iota((width, LANES), 1) // heads
        for i in range(GROUP):
            block_ref[i * width : (i + 1) * width, :] = jnp.where(owner == i, tiled, 0.0).astype(BF16)
        ones_ref[...] = jnp.full((width, width), 1.0 / width, BF16)

    gain = gain_ref[...][None, :]
    keys = x_ref.shape[1]
    owner = iota((keys, LANES), 1) // heads
    for q in range(STACK):
        lanes = slice(q * LANES, (q + 1) * LANES)
        spread_all = jnp.zeros((keys, LANES), F32)
        for i in range(GROUP):
            x = x_ref[q * GROUP + i]
            center = x.astype(F32) - dot(x, ones_ref[...])
            spread = lax.rsqrt(jnp.sum(center * center, axis=1, keepdims=True) * (1.0 / width) + EPS)
            standard = center * spread
            standard_ref[q * GROUP + i] = standard.astype(BF16)
            normed_ref[q * keys : (q + 1) * keys, i * width : (i + 1) * width] = (standard * gain).astype(BF16)
            spread_all = jnp.where(owner == i, spread, spread_all)
        spread_ref[:, lanes] = spread_all
    bias = dot(normed_ref[...], block_ref[...])
    for q in range(STACK):
        bias_ref[:, q * LANES : (q + 1) * LANES] = bias[q * keys : (q + 1) * keys]


def pair_forward(pair, gain, weight, first, count, previous=(), after=()):
    rows, keys, width = pair.shape
    heads = weight.shape[0]
    lanes = rows * heads
    outs = (
        jax.ShapeDtypeStruct((keys, lanes), F32),
        jax.ShapeDtypeStruct((keys, lanes), F32),
        jax.ShapeDtypeStruct(pair.shape, BF16),
    )
    before = tuple(previous)
    others = before + tuple(after)
    return pl.pallas_call(
        pair_kernel,
        grid=(count // STACK,),
        in_specs=[
            pl.BlockSpec((STACK * GROUP, keys, width), lambda g: (g + first // STACK, 0, 0)),
            whole(gain),
            whole(weight),
        ]
        + [pl.BlockSpec(memory_space=pl.ANY)] * len(others),
        out_specs=(
            pl.BlockSpec((keys, STACK * LANES), lambda g: (0, g + first // STACK)),
            pl.BlockSpec((keys, STACK * LANES), lambda g: (0, g + first // STACK)),
            pl.BlockSpec((STACK * GROUP, keys, width), lambda g: (g + first // STACK, 0, 0)),
        ),
        out_shape=outs,
        scratch_shapes=[
            pltpu.VMEM((GROUP * width, LANES), BF16),
            pltpu.VMEM((width, width), BF16),
            pltpu.VMEM((STACK * keys, GROUP * width), BF16),
        ],
        input_output_aliases={3 + i: i for i in range(len(before))},
        compiler_params=pltpu.CompilerParams(vmem_limit_bytes=56 * MIB),
        cost_estimate=pl.CostEstimate(
            flops=count * GROUP * keys * width * 5000, bytes_accessed=count * GROUP * keys * width * 5, transcendentals=0
        ),
        name="pair_forward",
    )(pair, gain, weight, *others)


def atom_kernel(
    left_ref, own_ref, right_ref, gain_ref, project_ref, merge_ref, up_ref,
    counts_ref, single_ref, token_gain_ref, weight_ref, cotangent_ref, _,
    hidden_ref, state_ref, normed_ref, send_ref, key_ref, value_ref, query_ref, attended_ref,
):
    atoms, width = own_ref.shape
    tokens = single_ref.shape[0]
    rows, columns = lax.axis_size("row"), lax.axis_size("col")
    first = (lax.axis_index("row") * columns + lax.axis_index("col")) * atoms
    feats = jnp.concatenate(
        [left_ref[atoms - LEFT :, :], own_ref[...], right_ref[:RIGHT, :]], axis=0
    )
    normed = normalize(feats.astype(F32), gain_ref[...][None, :]).astype(BF16)
    projected = dot(normed, project_ref[...]).astype(BF16)
    query_ref[...] = projected[LEFT : LEFT + atoms, :width]
    key_ref[...] = projected[:, width : 2 * width]
    value_ref[...] = projected[:, 2 * width :]
    size = width // ATOM_HEADS
    stacked = ATOM_HEADS * WINDOW
    lane_head = iota((stacked, width), 1) // size
    row_head = iota((stacked, width), 0) // WINDOW
    mask = lane_head == row_head
    key_index = iota((stacked, KEYS), 1)
    total = rows * columns * atoms
    for b in range(atoms // WINDOW):
        at = b * WINDOW
        queries = jnp.concatenate([query_ref[at : at + WINDOW, :]] * ATOM_HEADS, axis=0)
        queries = jnp.where(mask, queries.astype(F32), 0.0).astype(BF16)
        scores = dot_nt(queries, key_ref[at : at + KEYS, :]) / math.sqrt(size)
        position = first - LEFT + at + key_index
        scores = jnp.where((position >= 0) & (position < total), scores, NEGATIVE)
        weights = jnp.exp(scores - jnp.max(scores, axis=1, keepdims=True))
        row_total = jnp.sum(weights, axis=1, keepdims=True)
        mixture = dot(weights.astype(BF16), value_ref[at : at + KEYS, :]) / row_total
        mixture = jnp.where(mask, mixture, 0.0)
        joined = mixture[:WINDOW]
        for h in range(1, ATOM_HEADS):
            joined = joined + mixture[h * WINDOW : (h + 1) * WINDOW]
        attended_ref[at : at + WINDOW, :] = joined.astype(BF16)
    hidden = (own_ref[...].astype(F32) + dot(attended_ref[...], merge_ref[...])).astype(BF16)
    hidden_ref[...] = hidden
    lifted = jnp.maximum(dot(hidden, up_ref[...]), 0.0).astype(BF16)
    counts_row = counts_ref[...].astype(F32)
    square = jnp.broadcast_to(counts_row, (tokens, tokens))
    above = iota((tokens, tokens), 0)
    below = iota((tokens, tokens), 1)
    counts_col = jnp.sum(jnp.where(above == below, square, 0.0), axis=1, keepdims=True)
    ends = jnp.sum(jnp.where(below <= above, square, 0.0), axis=1, keepdims=True)
    atom = iota((tokens, atoms), 1).astype(F32)
    member = ((atom < ends) & (atom >= ends - counts_col)).astype(F32).astype(BF16)
    state = dot(member, lifted) / counts_col + single_ref[...].astype(F32)
    state_ref[...] = state
    token_normed = normalize(state, token_gain_ref[...][None, :]).astype(BF16)
    normed_ref[...] = token_normed
    turned = jnp.transpose(
        jnp.concatenate([cotangent_ref[...], jnp.zeros((LANES - 3, atoms), F32)], axis=0)
    )
    position_weight = weight_ref[...].astype(F32)
    grad_hidden = turned[:, 0:1] * position_weight[0:1, :]
    for k in range(1, 3):
        grad_hidden = grad_hidden + turned[:, k : k + 1] * position_weight[k : k + 1, :]
    grad_tokens = dot(member, grad_hidden.astype(BF16)).astype(BF16)
    packed = jnp.concatenate([token_normed, grad_tokens], axis=1)
    for c in range(send_ref.shape[0]):
        send_ref[c] = packed


def whole(array):
    zeros = (0,) * array.ndim
    return pl.BlockSpec(array.shape, lambda *_: zeros)


def atom_stage(left, own, right, gain, project, merge, up, counts, single, token_gain, weight, cotangent, copies, after):
    atoms, width = own.shape
    tokens, token_width = single.shape
    arrays = (left, own, right, gain, project, merge, up, counts, single, token_gain, weight, cotangent)
    outs = (
        jax.ShapeDtypeStruct((atoms, width), BF16),
        jax.ShapeDtypeStruct((tokens, token_width), F32),
        jax.ShapeDtypeStruct((tokens, token_width), BF16),
        jax.ShapeDtypeStruct((copies, tokens, token_width + width), BF16),
    )
    return pl.pallas_call(
        atom_kernel,
        grid=(1,),
        in_specs=[whole(a) for a in arrays]
        + [pl.BlockSpec(memory_space=pl.ANY)],
        out_specs=tuple(whole(a) for a in outs),
        out_shape=outs,
        scratch_shapes=[
            pltpu.VMEM((LEFT + atoms + RIGHT, width), BF16),
            pltpu.VMEM((LEFT + atoms + RIGHT, width), BF16),
            pltpu.VMEM((atoms, width), BF16),
            pltpu.VMEM((atoms, width), BF16),
        ],
        compiler_params=pltpu.CompilerParams(vmem_limit_bytes=56 * MIB),
        cost_estimate=pl.CostEstimate(flops=400 * MIB, bytes_accessed=2 * MIB, transcendentals=0),
        name="atom_stage",
    )(*arrays, after)


def query_kernel(rows_ref, project_ref, down_ref, merge_ref, query_ref, mix_ref):
    width = project_ref.shape[0]
    rows = rows_ref[...]
    query_ref[...] = dot(rows[:, :width], project_ref[...]).astype(BF16)
    update = dot_nt(rows[:, width:], down_ref[...]).astype(BF16)
    mix_ref[...] = dot_nt(update, merge_ref[...]).astype(BF16)


def query_stage(rows, project, down, merge):
    count = rows.shape[0]
    width = project.shape[0]
    out = jax.ShapeDtypeStruct((count, width), BF16)
    return pl.pallas_call(
        query_kernel,
        grid=(1,),
        in_specs=[whole(rows), pl.BlockSpec((width, width), lambda g: (0, 0)), whole(down), whole(merge)],
        out_specs=(whole(out), whole(out)),
        out_shape=(out, out),
        compiler_params=pltpu.CompilerParams(vmem_limit_bytes=24 * MIB),
        cost_estimate=pl.CostEstimate(flops=400 * MIB, bytes_accessed=4 * MIB, transcendentals=0),
        name="query_stage",
    )(rows, project, down, merge)


def attend_kernel(
    rows_ref, key_project_ref, value_project_ref, query_ref, mix_ref,
    bias_ref, spread_ref,
    weight_ref, grad_ref, small_ref, send_ref, key_ref, value_ref,
):
    step = pl.program_id(0)
    width = key_project_ref.shape[0]
    heads = 16
    stat_rows = 2 * 8

    @pl.when(step == 0)
    def _():
        rows = rows_ref[...]
        key_ref[...] = dot(rows, key_project_ref[...]).astype(BF16)
        value_ref[...] = dot(rows, value_project_ref[...]).astype(BF16)

    mask = head_mask(heads, width, heads)
    rows = query_ref.shape[0]

    def expanded(ref):
        spread_out = ref[...].astype(F32)[:, None, :] * mask[None]
        return spread_out.reshape(rows * heads, width).astype(BF16)

    keys = key_ref[...]
    values = value_ref[...]
    scores = dot_nt(keys, expanded(query_ref)) / math.sqrt(width // heads) + bias_ref[...]
    grad_probs = dot_nt(values, expanded(mix_ref))
    row_max = jnp.max(scores, axis=0, keepdims=True)
    weights = jnp.exp(scores - row_max)
    row_total = jnp.sum(weights, axis=0, keepdims=True)
    rounded = weights.astype(BF16)
    inner = jnp.sum(rounded.astype(F32) * grad_probs, axis=0, keepdims=True)
    weight_ref[...] = weights * spread_ref[...]
    grad_ref[...] = grad_probs
    small_ref[...] = (bias_ref[...] * (1.0 / LANES)).astype(BF16)
    per = rows * heads // LANES
    for k, stat in enumerate((row_max, row_total, inner)):
        for p in range(per):
            send_ref[0, pl.ds(k * stat_rows + step * per + p, 1), :] = stat[:, p * LANES : (p + 1) * LANES]
    mixture = dot_tn(rounded, values).reshape(rows, heads, width) * mask[None]
    part = jnp.sum(mixture, axis=1)
    for t in range(width // LANES):
        at = 3 * stat_rows + t * rows
        send_ref[step, at : at + rows, :] = part[:, t * LANES : (t + 1) * LANES]

    @pl.when(step == pl.num_programs(0) - 1)
    def _():
        stats = send_ref[0, : 3 * stat_rows, :]
        for c in range(1, send_ref.shape[0]):
            send_ref[c, : 3 * stat_rows, :] = stats


def attend_stage(key_rows, project, query, mix, bias, spread, owners):
    keys, lanes = bias.shape
    count, width = query.shape
    rows = count // owners
    chunk = lanes // owners
    stat_rows = 3 * lanes // LANES
    payload = jax.ShapeDtypeStruct((owners, stat_rows + rows * width // LANES, LANES), F32)
    tile = pl.BlockSpec((keys, chunk), lambda g: (0, g))
    return pl.pallas_call(
        attend_kernel,
        grid=(owners,),
        in_specs=[
            whole(key_rows),
            pl.BlockSpec((width, width), lambda g: (0, 1)),
            pl.BlockSpec((width, width), lambda g: (0, 2)),
            pl.BlockSpec((rows, width), lambda g: (g, 0)),
            pl.BlockSpec((rows, width), lambda g: (g, 0)),
            tile,
            tile,
        ],
        out_specs=(tile, tile, tile, whole(payload)),
        out_shape=(
            jax.ShapeDtypeStruct((keys, lanes), F32),
            jax.ShapeDtypeStruct((keys, lanes), F32),
            jax.ShapeDtypeStruct((keys, lanes), BF16),
            payload,
        ),
        scratch_shapes=[pltpu.VMEM((keys, width), BF16), pltpu.VMEM((keys, width), BF16)],
        compiler_params=pltpu.CompilerParams(vmem_limit_bytes=32 * MIB),
        cost_estimate=pl.CostEstimate(flops=3000 * MIB, bytes_accessed=12 * MIB, transcendentals=0),
        name="attend_stage",
    )(key_rows, project, project, query, mix, bias, spread)


def gradient_kernel(
    weight_ref, grad_ref, small_ref, standard_ref, received_ref, own_ref, gain_ref, bias_weight_ref,
    out_ref, block_ref, ones_ref, factor_ref, inner_ref,
):
    step = pl.program_id(0)
    heads, width = bias_weight_ref.shape
    rows = factor_ref.shape[0]

    @pl.when(step == 0)
    def _():
        lane = iota((heads, LANES), 1)
        repeat = (lane % heads == iota((heads, LANES), 0)).astype(BF16)
        tiled = dot_tn(repeat, bias_weight_ref[...]) * gain_ref[...][None, :]
        tiled = tiled - jnp.mean(tiled, axis=1, keepdims=True)
        high, low = split(tiled)
        owner = iota((LANES, width), 0) // heads
        for i in range(GROUP):
            mine = owner == i
            at = slice(i * width, (i + 1) * width)
            block_ref[:LANES, at] = jnp.where(mine, high.astype(F32), 0.0).astype(BF16)
            block_ref[LANES:, at] = jnp.where(mine, low.astype(F32), 0.0).astype(BF16)
            ones = jnp.where(mine, 1.0, 0.0).astype(BF16)
            ones_ref[:LANES, at] = ones
            ones_ref[LANES:, at] = ones
        parts = received_ref.shape[0]
        top = received_ref[0, :rows, :]
        for s in range(1, parts):
            top = jnp.maximum(top, received_ref[s, :rows, :])
        total = jnp.zeros_like(top)
        inner = jnp.zeros_like(top)
        for s in range(parts):
            scale = jnp.exp(received_ref[s, :rows, :] - top)
            total = total + scale * received_ref[s, rows : 2 * rows, :]
            inner = inner + scale * received_ref[s, 2 * rows : 3 * rows, :]
        factor_ref[...] = jnp.exp(own_ref[0, :rows, :] - top) / total
        inner_ref[...] = inner / total

    keys = weight_ref.shape[0]
    lefts, rights = [], []
    for q in range(STACK):
        lanes = slice(q * LANES, (q + 1) * LANES)
        factor = factor_ref[pl.ds(step * STACK + q, 1), :]
        inner = inner_ref[pl.ds(step * STACK + q, 1), :]
        grad = weight_ref[:, lanes] * factor * (grad_ref[:, lanes] - inner)
        rounded = grad.astype(BF16)
        lefts.append(jnp.concatenate([rounded, rounded], axis=1))
        rights.append(jnp.concatenate(split(grad * small_ref[:, lanes].astype(F32)), axis=1))
    left = jnp.concatenate(lefts, axis=0)
    right = jnp.concatenate(rights, axis=0)
    for i in range(0, GROUP, 2):
        at = slice(i * width, (i + 2) * width)
        direct = dot(left, block_ref[:, at])
        along = dot(right, ones_ref[:, at])
        for q in range(STACK):
            for k in range(2):
                part = (slice(q * keys, (q + 1) * keys), slice(k * width, (k + 1) * width))
                r = q * GROUP + i + k
                out_ref[r] = (direct[part] - standard_ref[r].astype(F32) * along[part]).astype(BF16)


def gradient_stage(weights, grad, small, standard, received, own, gain, bias_weight):
    rows, keys, width = standard.shape
    tile = pl.BlockSpec((keys, STACK * LANES), lambda g: (0, g))
    block = pl.BlockSpec((STACK * GROUP, keys, width), lambda g: (g, 0, 0))
    return pl.pallas_call(
        gradient_kernel,
        grid=(rows // GROUP // STACK,),
        in_specs=[tile, tile, tile, block, whole(received), whole(own), whole(gain), whole(bias_weight)],
        out_specs=block,
        out_shape=jax.ShapeDtypeStruct(standard.shape, BF16),
        scratch_shapes=[
            pltpu.VMEM((2 * LANES, GROUP * width), BF16),
            pltpu.VMEM((2 * LANES, GROUP * width), BF16),
            pltpu.VMEM((rows // GROUP, LANES), F32),
            pltpu.VMEM((rows // GROUP, LANES), F32),
        ],
        compiler_params=pltpu.CompilerParams(vmem_limit_bytes=32 * MIB),
        cost_estimate=pl.CostEstimate(flops=16000 * MIB, bytes_accessed=22 * MIB, transcendentals=0),
        name="gradient_stage",
    )(weights, grad, small, standard, received, own, gain, bias_weight)


def update_kernel(
    received_ref, state_ref, hidden_ref, counts_ref, merge_ref, down_ref, weight_ref,
    positions_ref, update_ref,
):
    column = lax.axis_index("col")
    tokens, width = state_ref.shape
    heads = 16
    parts = received_ref.shape[0]
    stat_rows = (received_ref.shape[1] - tokens * width // LANES) // 3
    halves = tokens // GROUP

    def stats(kind, part):
        at = kind * stat_rows + column * halves
        return [received_ref[part, pl.ds(at + p, 1), :] for p in range(halves)]

    maxima = [stats(0, s) for s in range(parts)]
    totals = [stats(1, s) for s in range(parts)]
    sub = iota((tokens, LANES), 0)
    lane = iota((tokens, LANES), 1)
    scales = [[] for _ in range(parts)]
    for p in range(halves):
        top = maxima[0][p]
        for s in range(1, parts):
            top = jnp.maximum(top, maxima[s][p])
        exps = [jnp.exp(maxima[s][p] - top) for s in range(parts)]
        total = exps[0] * totals[0][p]
        for s in range(1, parts):
            total = total + exps[s] * totals[s][p]
        for s in range(parts):
            scales[s].append(exps[s] / total)
    mine = lane // heads == sub % GROUP
    rows = []
    for s in range(parts):
        picked = jnp.zeros((tokens, LANES), F32)
        for p in range(halves):
            picked = jnp.where(sub // GROUP == p, jnp.broadcast_to(scales[s][p], (tokens, LANES)), picked)
        rows.append(jnp.where(mine, picked, 0.0))
    stacked = jnp.concatenate(rows, axis=0)
    spread_out = head_mask(LANES, width, heads).astype(BF16)
    high, low = split(stacked)
    rest = stacked - high.astype(F32) - low.astype(F32)
    scale = dot(high, spread_out) + dot(low, spread_out) + dot(rest.astype(BF16), spread_out)
    pieces = []
    for t in range(width // LANES):
        at = 3 * stat_rows + t * tokens
        piece = jnp.zeros((tokens, LANES), F32)
        for s in range(parts):
            factor = scale[s * tokens : (s + 1) * tokens, t * LANES : (t + 1) * LANES]
            piece = piece + factor * received_ref[s, at : at + tokens, :]
        pieces.append(piece.astype(BF16))
    attention = jnp.concatenate(pieces, axis=1)
    update = (state_ref[...] + dot(attention, merge_ref[...])).astype(BF16)
    update_ref[...] = update
    lowered = dot(update, down_ref[...]).astype(BF16)
    atoms = hidden_ref.shape[0]
    counts_row = counts_ref[...].astype(F32)
    square = jnp.broadcast_to(counts_row, (tokens, tokens))
    above = iota((tokens, tokens), 0)
    below = iota((tokens, tokens), 1)
    counts_col = jnp.sum(jnp.where(above == below, square, 0.0), axis=1, keepdims=True)
    ends = jnp.sum(jnp.where(below <= above, square, 0.0), axis=1, keepdims=True)
    atom = iota((tokens, atoms), 1).astype(F32)
    member = ((atom < ends) & (atom >= ends - counts_col)).astype(F32).astype(BF16)
    hidden_next = (hidden_ref[...].astype(F32) + dot_tn(member, lowered)).astype(BF16)
    positions_ref[...] = dot_nt(weight_ref[...], hidden_next)


def update_stage(received, state, hidden, counts, merge, down, weight):
    tokens, width = state.shape
    arrays = (received, state, hidden, counts, merge, down, weight)
    outs = (
        jax.ShapeDtypeStruct((weight.shape[0], hidden.shape[0]), F32),
        jax.ShapeDtypeStruct((tokens, width), BF16),
    )
    return pl.pallas_call(
        update_kernel,
        grid=(1,),
        in_specs=[whole(a) for a in arrays],
        out_specs=tuple(whole(a) for a in outs),
        out_shape=outs,
        compiler_params=pltpu.CompilerParams(vmem_limit_bytes=24 * MIB),
        cost_estimate=pl.CostEstimate(flops=100 * MIB, bytes_accessed=3 * MIB, transcendentals=0),
        name="update_stage",
    )(*arrays)


def per_device(
    atom_feats, atom_gain, atom_project, atom_merge, atom_up, token_counts, token_single, token_gain,
    token_project, token_merge, pair_state, pair_gain, bias_weight, atom_down, position_weight,
    position_cotangent,
):
    both = ("row", "col")
    rows, columns = lax.axis_size("row"), lax.axis_size("col")
    devices = rows * columns
    left = lax.ppermute(atom_feats, both, [(i, i + 1) for i in range(devices - 1)])
    right = lax.ppermute(atom_feats, both, [(i + 1, i) for i in range(devices - 1)])
    gain = pair_gain
    bias_turned = bias_weight.T
    groups = pair_state.shape[0] // GROUP
    cuts = (0, STACK, groups - STACK, groups)
    pair_part = pair_forward(pair_state, gain, bias_turned, 0, cuts[1])
    hidden, state, token_normed, send = atom_stage(
        left, atom_feats, right, atom_gain, atom_project, atom_merge, atom_up,
        token_counts, token_single, token_gain, position_weight, position_cotangent, columns, pair_part[0],
    )
    pair_part = pair_forward(pair_state, gain, bias_turned, cuts[1], cuts[2] - cuts[1], pair_part, (send,))
    route = [(c * rows + r, r * columns + c) for r in range(rows) for c in range(columns)]
    block = lax.ppermute(token_normed, both, route)
    gathered = lax.all_to_all(send, "col", 0, 0)
    gathered = gathered.reshape(-1, gathered.shape[-1])
    key_rows = lax.all_to_all(jnp.broadcast_to(block[None], (rows,) + block.shape), "row", 0, 0)
    key_rows = key_rows.reshape(-1, key_rows.shape[-1])
    query, mix = query_stage(gathered, token_project, atom_down, token_merge)
    bias, spread, standard = pair_forward(
        pair_state, gain, bias_turned, cuts[2], cuts[3] - cuts[2], pair_part, (gathered,)
    )
    weights, grad, small, payload = attend_stage(
        key_rows, token_project, query, mix, bias, spread, columns
    )
    received = lax.all_to_all(payload, "col", 0, 0)
    positions, token_update = update_stage(
        received, state, hidden, token_counts, token_merge, atom_down, position_weight,
    )
    pair_grad = gradient_stage(weights, grad, small, standard, received, payload, gain, bias_turned)
    return (positions, token_update, pair_grad)


def solution(mesh):
    placed = (
        P(("row", "col"), None), P(), P(), P(), P(), P(("row", "col"), None), P(("row", "col"), None), P(),
        P(), P(), P("row", "col", None), P(), P(), P(), P(), P(None, ("row", "col")),
    )
    return jax.shard_map(
        per_device,
        mesh=mesh,
        in_specs=placed,
        out_specs=(P(None, ("row", "col")), P(("row", "col"), None), P("row", "col", None)),
        check_vma=False,
    )
```

```python
import math

import jax
import jax.numpy as jnp
from jax import lax
from jax.experimental import pallas as pl
from jax.experimental.pallas import tpu as pltpu
from jax.sharding import PartitionSpec as P

ATOM_HEADS = 4
TOKEN_HEADS = 16
EPS = 1e-05
NEGATIVE = -1e30
LEFT, RIGHT = 48, 80
WINDOW = 32
KEYS = 128
LANES = 128
GROUP = 8
TERM_SLOTS = 8
KINDS = 3
ATTEND_STACK = 4
PAIR_STACK = 2
STACK = 4
F32 = jnp.float32
BF16 = jnp.bfloat16
NT = (((1,), (1,)), ((), ()))
TN = (((0,), (0,)), ((), ()))
MIB = 1 << 20
PAIR_LIMIT = 56
ATOM_LIMIT = 40
ATTEND_LIMIT = 46
GRADIENT_LIMIT = 32


def iota(shape, axis):
    return lax.broadcasted_iota(jnp.int32, shape, axis)


def dot(a, b):
    return jnp.dot(a, b, preferred_element_type=F32)


def dot_nt(a, b):
    return lax.dot_general(a, b, NT, preferred_element_type=F32)


def dot_tn(a, b):
    return lax.dot_general(a, b, TN, preferred_element_type=F32)


def split(value):
    high = value.astype(BF16)
    return high, (value - high.astype(F32)).astype(BF16)


def normalize(values, gain):
    center = values - jnp.mean(values, axis=-1, keepdims=True)
    spread = lax.rsqrt(jnp.mean(center * center, axis=-1, keepdims=True) + EPS)
    return center * spread * gain


def head_mask(rows, width, heads):
    size = width // heads
    head = iota((rows, width), 0) % heads
    column = iota((rows, width), 1)
    return ((column >= head * size) & (column < (head + 1) * size)).astype(F32)


def pair_kernel(x_ref, gain_ref, weight_ref, *rest):
    terms_ref, standard_ref, block_ref, ones_ref, normed_ref = rest[-5:]
    heads = weight_ref.shape[0]
    width = x_ref.shape[2]

    @pl.when(pl.program_id(0) == 0)
    def _():
        lane = iota((heads, LANES), 1)
        repeat = (lane % heads == iota((heads, LANES), 0)).astype(BF16)
        tiled = dot_tn(weight_ref[...], repeat)
        owner = iota((width, LANES), 1) // heads
        for i in range(GROUP):
            block_ref[i * width : (i + 1) * width, :] = jnp.where(owner == i, tiled, 0.0).astype(BF16)
        ones_ref[...] = jnp.full((width, width), 1.0 / width, BF16)

    gain = gain_ref[...][None, :]
    keys = x_ref.shape[1]
    owner = iota((keys, LANES), 1) // heads
    for q in range(PAIR_STACK):
        lanes = slice(q * LANES, (q + 1) * LANES)
        spread_all = jnp.zeros((keys, LANES), F32)
        for i in range(GROUP):
            x = x_ref[q * GROUP + i]
            center = x.astype(F32) - dot(x, ones_ref[...])
            spread = lax.rsqrt(jnp.sum(center * center, axis=1, keepdims=True) * (1.0 / width) + EPS)
            standard = center * spread
            standard_ref[q * GROUP + i] = standard.astype(BF16)
            normed_ref[q * keys : (q + 1) * keys, i * width : (i + 1) * width] = (standard * gain).astype(BF16)
            spread_all = jnp.where(owner == i, spread, spread_all)
        terms_ref[1, :, lanes] = spread_all
    bias = dot(normed_ref[...], block_ref[...])
    for q in range(PAIR_STACK):
        terms_ref[0, :, q * LANES : (q + 1) * LANES] = bias[q * keys : (q + 1) * keys]


def pair_forward(pair, gain, weight, first, count, previous=(), after=()):
    rows, keys, width = pair.shape
    heads = weight.shape[0]
    lanes = rows * heads
    outs = (
        jax.ShapeDtypeStruct((TERM_SLOTS, keys, lanes), F32),
        jax.ShapeDtypeStruct(pair.shape, BF16),
    )
    before = tuple(previous)
    others = before + tuple(after)
    return pl.pallas_call(
        pair_kernel,
        grid=(count // PAIR_STACK,),
        in_specs=[
            pl.BlockSpec((PAIR_STACK * GROUP, keys, width), lambda g: (g + first // PAIR_STACK, 0, 0)),
            whole(gain),
            whole(weight),
        ]
        + [pl.BlockSpec(memory_space=pl.ANY)] * len(others),
        out_specs=(
            pl.BlockSpec((2, keys, PAIR_STACK * LANES), lambda g: (0, 0, g + first // PAIR_STACK)),
            pl.BlockSpec((PAIR_STACK * GROUP, keys, width), lambda g: (g + first // PAIR_STACK, 0, 0)),
        ),
        out_shape=outs,
        scratch_shapes=[
            pltpu.VMEM((GROUP * width, LANES), BF16),
            pltpu.VMEM((width, width), BF16),
            pltpu.VMEM((PAIR_STACK * keys, GROUP * width), BF16),
        ],
        input_output_aliases={3 + i: i for i in range(len(before))},
        compiler_params=pltpu.CompilerParams(vmem_limit_bytes=PAIR_LIMIT * MIB),
        cost_estimate=pl.CostEstimate(
            flops=count * GROUP * keys * width * 5000, bytes_accessed=count * GROUP * keys * width * 5, transcendentals=0
        ),
        name="pair_forward",
    )(pair, gain, weight, *others)


def atom_kernel(
    left_ref, own_ref, right_ref, gain_ref, project_ref, merge_ref, up_ref,
    counts_ref, single_ref, token_gain_ref, weight_ref, cotangent_ref, _,
    hidden_ref, state_ref, packed_ref, send_ref, key_ref, value_ref, query_ref, attended_ref,
):
    atoms, width = own_ref.shape
    tokens = single_ref.shape[0]
    rows, columns = lax.axis_size("row"), lax.axis_size("col")
    first = (lax.axis_index("row") * columns + lax.axis_index("col")) * atoms
    feats = jnp.concatenate(
        [left_ref[atoms - LEFT :, :], own_ref[...], right_ref[:RIGHT, :]], axis=0
    )
    normed = normalize(feats.astype(F32), gain_ref[...][None, :]).astype(BF16)
    projected = dot(normed, project_ref[...]).astype(BF16)
    query_ref[...] = projected[LEFT : LEFT + atoms, :width]
    key_ref[...] = projected[:, width : 2 * width]
    value_ref[...] = projected[:, 2 * width :]
    size = width // ATOM_HEADS
    stacked = ATOM_HEADS * WINDOW
    lane_head = iota((stacked, width), 1) // size
    row_head = iota((stacked, width), 0) // WINDOW
    mask = lane_head == row_head
    key_index = iota((stacked, KEYS), 1)
    total = rows * columns * atoms
    for b in range(atoms // WINDOW):
        at = b * WINDOW
        queries = jnp.concatenate([query_ref[at : at + WINDOW, :]] * ATOM_HEADS, axis=0)
        queries = jnp.where(mask, queries.astype(F32), 0.0).astype(BF16)
        scores = dot_nt(queries, key_ref[at : at + KEYS, :]) / math.sqrt(size)
        position = first - LEFT + at + key_index
        scores = jnp.where((position >= 0) & (position < total), scores, NEGATIVE)
        weights = jnp.exp(scores - jnp.max(scores, axis=1, keepdims=True))
        row_total = jnp.sum(weights, axis=1, keepdims=True)
        mixture = dot(weights.astype(BF16), value_ref[at : at + KEYS, :]) / row_total
        mixture = jnp.where(mask, mixture, 0.0)
        joined = mixture[:WINDOW]
        for h in range(1, ATOM_HEADS):
            joined = joined + mixture[h * WINDOW : (h + 1) * WINDOW]
        attended_ref[at : at + WINDOW, :] = joined.astype(BF16)
    hidden = (own_ref[...].astype(F32) + dot(attended_ref[...], merge_ref[...])).astype(BF16)
    hidden_ref[...] = hidden
    lifted = jnp.maximum(dot(hidden, up_ref[...]), 0.0).astype(BF16)
    counts_row = counts_ref[...].astype(F32)
    square = jnp.broadcast_to(counts_row, (tokens, tokens))
    above = iota((tokens, tokens), 0)
    below = iota((tokens, tokens), 1)
    counts_col = jnp.sum(jnp.where(above == below, square, 0.0), axis=1, keepdims=True)
    ends = jnp.sum(jnp.where(below <= above, square, 0.0), axis=1, keepdims=True)
    atom = iota((tokens, atoms), 1).astype(F32)
    member = ((atom < ends) & (atom >= ends - counts_col)).astype(F32).astype(BF16)
    state = dot(member, lifted) / counts_col + single_ref[...].astype(F32)
    state_ref[...] = state
    token_normed = normalize(state, token_gain_ref[...][None, :]).astype(BF16)
    turned = jnp.transpose(
        jnp.concatenate([cotangent_ref[...], jnp.zeros((LANES - 3, atoms), F32)], axis=0)
    )
    position_weight = weight_ref[...].astype(F32)
    grad_hidden = turned[:, 0:1] * position_weight[0:1, :]
    for k in range(1, 3):
        grad_hidden = grad_hidden + turned[:, k : k + 1] * position_weight[k : k + 1, :]
    grad_tokens = dot(member, grad_hidden.astype(BF16)).astype(BF16)
    tiles = [token_normed[:, t * LANES : (t + 1) * LANES] for t in range(token_normed.shape[1] // LANES)]
    block = jnp.concatenate(tiles, axis=0)
    packed_ref[...] = jnp.concatenate([block, grad_tokens], axis=0)
    for c in range(send_ref.shape[0]):
        send_ref[c] = block


def whole(array):
    zeros = (0,) * array.ndim
    return pl.BlockSpec(array.shape, lambda *_: zeros)


def atom_stage(left, own, right, gain, project, merge, up, counts, single, token_gain, weight, cotangent, copies, after):
    atoms, width = own.shape
    tokens, token_width = single.shape
    arrays = (left, own, right, gain, project, merge, up, counts, single, token_gain, weight, cotangent)
    outs = (
        jax.ShapeDtypeStruct((atoms, width), BF16),
        jax.ShapeDtypeStruct((tokens, token_width), F32),
        jax.ShapeDtypeStruct((tokens * token_width // LANES + tokens, LANES), BF16),
        jax.ShapeDtypeStruct((copies, tokens * token_width // LANES, LANES), BF16),
    )
    return pl.pallas_call(
        atom_kernel,
        grid=(1,),
        in_specs=[whole(a) for a in arrays]
        + [pl.BlockSpec(memory_space=pl.ANY)],
        out_specs=tuple(whole(a) for a in outs),
        out_shape=outs,
        scratch_shapes=[
            pltpu.VMEM((LEFT + atoms + RIGHT, width), BF16),
            pltpu.VMEM((LEFT + atoms + RIGHT, width), BF16),
            pltpu.VMEM((atoms, width), BF16),
            pltpu.VMEM((atoms, width), BF16),
        ],
        compiler_params=pltpu.CompilerParams(vmem_limit_bytes=ATOM_LIMIT * MIB),
        cost_estimate=pl.CostEstimate(flops=400 * MIB, bytes_accessed=2 * MIB, transcendentals=0),
        name="atom_stage",
    )(*arrays, after)


def attend_kernel(
    gathered_ref, down_ref, project_hbm, merge_hbm, terms_hbm,
    weight_ref, grad_ref, small_ref, send_ref,
    query_ref, mix_ref, key_ref, value_ref, stat_ref, project_ref, merge_ref, terms_ref,
    weight_semaphores, semaphores,
):
    step = pl.program_id(0)
    owners = send_ref.shape[0]
    steps = owners // ATTEND_STACK
    width = project_ref.shape[1]
    heads = TOKEN_HEADS
    chunk = weight_ref.shape[1]
    per = chunk // LANES
    stat_rows = steps * per
    part_rows = query_ref.shape[0] // owners
    part_lanes = chunk // ATTEND_STACK

    def terms_copy(at):
        lanes = pl.ds(pl.multiple_of(at * chunk, chunk), chunk)
        return pltpu.make_async_copy(terms_hbm.at[0:2, :, lanes], terms_ref.at[:, :, lanes], semaphores.at[at])

    @pl.when(step == 0)
    def _():
        thirds = [
            pltpu.make_async_copy(
                project_hbm.at[:, k * width : (k + 1) * width], project_ref.at[k], weight_semaphores.at[k]
            )
            for k in range(3)
        ]
        merge = pltpu.make_async_copy(merge_hbm, merge_ref, weight_semaphores.at[3])
        for copy in (*thirds, merge, terms_copy(0), terms_copy(1)):
            copy.start()
        tiles = width // LANES
        own = gathered_ref.shape[1] // (KINDS * tiles + 1)

        def tile(index):
            return gathered_ref[:, index * own : (index + 1) * own, :].reshape(-1, LANES)

        blocks = [
            jnp.concatenate([tile(k * tiles + t) for t in range(tiles)], axis=1) for k in range(KINDS)
        ]
        rows = jnp.concatenate(blocks[:-1], axis=0)
        update = dot_nt(tile(KINDS * tiles), down_ref[...]).astype(BF16)
        thirds[0].wait()
        query_ref[...] = dot(blocks[-1], project_ref[0]).astype(BF16)
        thirds[1].wait()
        key_ref[...] = dot(rows, project_ref[1]).astype(BF16)
        thirds[2].wait()
        value_ref[...] = dot(rows, project_ref[2]).astype(BF16)
        merge.wait()
        mix_ref[...] = dot_nt(update, merge_ref[...]).astype(BF16)

    @pl.when(step < steps - 2)
    def _():
        terms_copy(step + 2).start()

    terms_copy(step).wait()
    mask = head_mask(heads, width, heads)

    def expanded(ref, at):
        own = pl.ds(pl.multiple_of(at * part_rows, part_rows), part_rows)
        spread_out = ref[own, :].astype(F32)[:, None, :] * mask[None]
        return spread_out.reshape(part_rows * heads, width).astype(BF16)

    values = value_ref[...]
    all_rounded = []
    for sub in range(ATTEND_STACK):
        at = step * ATTEND_STACK + sub
        inside = slice(sub * part_lanes, (sub + 1) * part_lanes)
        lanes = pl.ds(pl.multiple_of(at * part_lanes, part_lanes), part_lanes)
        bias = terms_ref[0, :, lanes]
        scores = dot_nt(key_ref[...], expanded(query_ref, at)) / math.sqrt(width // heads) + bias
        grad_probs = dot_nt(values, expanded(mix_ref, at))
        row_max = jnp.max(scores, axis=0, keepdims=True).astype(BF16).astype(F32)
        weights = jnp.exp(scores - row_max)
        row_total = jnp.sum(weights, axis=0, keepdims=True)
        rounded = weights.astype(BF16)
        all_rounded.append(rounded)
        inner = jnp.sum(rounded.astype(F32) * grad_probs, axis=0, keepdims=True)
        weight_ref[:, inside] = (weights * terms_ref[1, :, lanes]).astype(BF16)
        grad_ref[:, inside] = grad_probs
        small_ref[:, inside] = (bias * (1.0 / LANES)).astype(BF16)
        for k, stat in enumerate((row_max, row_total, inner)):
            for p in range(part_lanes // LANES):
                row = k * stat_rows + at * (part_lanes // LANES) + p
                stat_ref[pl.ds(row, 1), :] = stat[:, p * LANES : (p + 1) * LANES]
    mixture = dot_tn(jnp.concatenate(all_rounded, axis=1), values).reshape(-1, heads, width) * mask[None]
    part = jnp.sum(mixture, axis=1).astype(BF16)
    for sub in range(ATTEND_STACK):
        for t in range(width // LANES):
            low = 5 * stat_rows + t * part_rows
            send_ref[step * ATTEND_STACK + sub, low : low + part_rows, :] = part[
                sub * part_rows : (sub + 1) * part_rows, t * LANES : (t + 1) * LANES
            ]

    @pl.when(step == steps - 1)
    def _():
        pieces = [stat_ref[:stat_rows, :].astype(BF16)]
        for k in (1, 2):
            pieces.extend(split(stat_ref[k * stat_rows : (k + 1) * stat_rows, :]))
        stats = jnp.concatenate(pieces, axis=0)
        for c in range(owners):
            send_ref[c, : 5 * stat_rows, :] = stats


def attend_stage(gathered, project, down, merge, terms, owners):
    _, keys, lanes = terms.shape
    width = project.shape[0]
    count = gathered.shape[0] * gathered.shape[1] // (KINDS * (width // LANES) + 1)
    rows = count // owners
    steps = owners // ATTEND_STACK
    chunk = lanes // steps
    stat_rows = lanes // LANES
    payload = jax.ShapeDtypeStruct((owners, 5 * stat_rows + rows * width // LANES, LANES), BF16)
    tile = pl.BlockSpec((keys, chunk), lambda g: (0, g))
    arrays = (gathered, down)
    return pl.pallas_call(
        attend_kernel,
        grid=(steps,),
        in_specs=[whole(a) for a in arrays] + [pl.BlockSpec(memory_space=pl.ANY)] * 3,
        out_specs=(tile, tile, tile, whole(payload)),
        out_shape=(
            jax.ShapeDtypeStruct((keys, lanes), BF16),
            jax.ShapeDtypeStruct((keys, lanes), F32),
            jax.ShapeDtypeStruct((keys, lanes), BF16),
            payload,
        ),
        scratch_shapes=[
            pltpu.VMEM((count, width), BF16),
            pltpu.VMEM((count, width), BF16),
            pltpu.VMEM((keys, width), BF16),
            pltpu.VMEM((keys, width), BF16),
            pltpu.VMEM((3 * stat_rows, LANES), F32),
            pltpu.VMEM((3, width, width), BF16),
            pltpu.VMEM((width, width), BF16),
            pltpu.VMEM((2, keys, lanes), F32),
            pltpu.SemaphoreType.DMA((4,)),
            pltpu.SemaphoreType.DMA((steps,)),
        ],
        compiler_params=pltpu.CompilerParams(vmem_limit_bytes=ATTEND_LIMIT * MIB),
        cost_estimate=pl.CostEstimate(flops=8000 * MIB, bytes_accessed=12 * MIB, transcendentals=0),
        name="attend_stage",
    )(*arrays, project, merge, terms)


def combined(received_ref, rows):
    parts = received_ref.shape[0]

    def stat(part, index):
        return received_ref[part, index * rows : (index + 1) * rows, :].astype(F32)

    maxima = [stat(s, 0) for s in range(parts)]
    top = maxima[0]
    for s in range(1, parts):
        top = jnp.maximum(top, maxima[s])
    scales = [jnp.exp(value - top) for value in maxima]
    total = jnp.zeros_like(top)
    inner = jnp.zeros_like(top)
    for s in range(parts):
        total = total + scales[s] * (stat(s, 1) + stat(s, 2))
        inner = inner + scales[s] * (stat(s, 3) + stat(s, 4))
    return top, scales, total, inner


def update_tokens(
    received_ref, state_ref, hidden_ref, counts_ref, merge_ref, down_ref, weight_ref, positions_ref, update_ref,
    scales, total,
):
    column = lax.axis_index("col")
    tokens, width = state_ref.shape
    heads = TOKEN_HEADS
    parts = received_ref.shape[0]
    stat_rows = (received_ref.shape[1] - tokens * width // LANES) // 5
    halves = tokens // GROUP
    sub = iota((tokens, LANES), 0)
    mine = iota((tokens, LANES), 1) // heads == sub % GROUP
    stat_row = iota((stat_rows, LANES), 0)
    rows = []
    for s in range(parts):
        scale = scales[s] / total
        picked = jnp.zeros((tokens, LANES), F32)
        for p in range(halves):
            one = jnp.sum(jnp.where(stat_row == column * halves + p, scale, 0.0), axis=0, keepdims=True)
            picked = jnp.where(sub // GROUP == p, one, picked)
        rows.append(jnp.where(mine, picked, 0.0))
    stacked = jnp.concatenate(rows, axis=0)
    spread_out = head_mask(LANES, width, heads).astype(BF16)
    high, low = split(stacked)
    rest = stacked - high.astype(F32) - low.astype(F32)
    scale = dot(high, spread_out) + dot(low, spread_out) + dot(rest.astype(BF16), spread_out)
    pieces = []
    for t in range(width // LANES):
        at = 5 * stat_rows + t * tokens
        piece = jnp.zeros((tokens, LANES), F32)
        for s in range(parts):
            factor = scale[s * tokens : (s + 1) * tokens, t * LANES : (t + 1) * LANES]
            piece = piece + factor * received_ref[s, at : at + tokens, :].astype(F32)
        pieces.append(piece.astype(BF16))
    attention = jnp.concatenate(pieces, axis=1)
    update = (state_ref[...] + dot(attention, merge_ref[...])).astype(BF16)
    update_ref[...] = update
    lowered = dot(update, down_ref[...]).astype(BF16)
    atoms = hidden_ref.shape[0]
    counts_row = counts_ref[...].astype(F32)
    square = jnp.broadcast_to(counts_row, (tokens, tokens))
    above = iota((tokens, tokens), 0)
    below = iota((tokens, tokens), 1)
    counts_col = jnp.sum(jnp.where(above == below, square, 0.0), axis=1, keepdims=True)
    ends = jnp.sum(jnp.where(below <= above, square, 0.0), axis=1, keepdims=True)
    atom = iota((tokens, atoms), 1).astype(F32)
    member = ((atom < ends) & (atom >= ends - counts_col)).astype(F32).astype(BF16)
    hidden_next = (hidden_ref[...].astype(F32) + dot_tn(member, lowered)).astype(BF16)
    positions_ref[...] = dot_nt(weight_ref[...], hidden_next)


def gradient_kernel(
    weight_ref, grad_ref, small_ref, standard_ref, received_ref, own_ref, gain_ref, bias_weight_ref,
    state_ref, hidden_ref, counts_ref, merge_ref, down_ref, position_ref,
    out_ref, positions_ref, update_ref, block_ref, ones_ref, factor_ref, inner_ref,
):
    step = pl.program_id(0)
    heads, width = bias_weight_ref.shape
    rows = factor_ref.shape[0]

    @pl.when(step == 0)
    def _():
        lane = iota((heads, LANES), 1)
        repeat = (lane % heads == iota((heads, LANES), 0)).astype(BF16)
        tiled = dot_tn(repeat, bias_weight_ref[...]) * gain_ref[...][None, :]
        tiled = tiled - jnp.mean(tiled, axis=1, keepdims=True)
        high, low = split(tiled)
        owner = iota((LANES, width), 0) // heads
        for i in range(GROUP):
            mine = owner == i
            at = slice(i * width, (i + 1) * width)
            block_ref[:LANES, at] = jnp.where(mine, high.astype(F32), 0.0).astype(BF16)
            block_ref[LANES:, at] = jnp.where(mine, low.astype(F32), 0.0).astype(BF16)
            ones = jnp.where(mine, 1.0, 0.0).astype(BF16)
            ones_ref[:LANES, at] = ones
            ones_ref[LANES:, at] = ones
        top, scales, total, inner = combined(received_ref, rows)
        factor_ref[...] = jnp.exp(own_ref[0, :rows, :].astype(F32) - top) / total
        inner_ref[...] = inner / total
        update_tokens(
            received_ref, state_ref, hidden_ref, counts_ref, merge_ref, down_ref, position_ref,
            positions_ref, update_ref, scales, total,
        )

    keys = weight_ref.shape[0]
    lefts, rights = [], []
    for q in range(STACK):
        lanes = slice(q * LANES, (q + 1) * LANES)
        factor = factor_ref[pl.ds(step * STACK + q, 1), :]
        inner = inner_ref[pl.ds(step * STACK + q, 1), :]
        grad = weight_ref[:, lanes].astype(F32) * factor * (grad_ref[:, lanes] - inner)
        rounded = grad.astype(BF16)
        lefts.append(jnp.concatenate([rounded, rounded], axis=1))
        rights.append(jnp.concatenate(split(grad * small_ref[:, lanes].astype(F32)), axis=1))
    left = jnp.concatenate(lefts, axis=0)
    right = jnp.concatenate(rights, axis=0)
    for i in range(0, GROUP, 2):
        at = slice(i * width, (i + 2) * width)
        direct = dot(left, block_ref[:, at])
        along = dot(right, ones_ref[:, at])
        for q in range(STACK):
            for k in range(2):
                part = (slice(q * keys, (q + 1) * keys), slice(k * width, (k + 1) * width))
                r = q * GROUP + i + k
                out_ref[r] = (direct[part] - standard_ref[r].astype(F32) * along[part]).astype(BF16)


def gradient_stage(weights, grad, small, standard, received, own, gain, bias_weight, state, hidden, counts, merge, down, weight):
    rows, keys, width = standard.shape
    arrays = (received, own, gain, bias_weight, state, hidden, counts, merge, down, weight)
    outs = (
        jax.ShapeDtypeStruct((weight.shape[0], hidden.shape[0]), F32),
        jax.ShapeDtypeStruct(state.shape, BF16),
    )
    tile = pl.BlockSpec((keys, STACK * LANES), lambda g: (0, g))
    block = pl.BlockSpec((STACK * GROUP, keys, width), lambda g: (g, 0, 0))
    return pl.pallas_call(
        gradient_kernel,
        grid=(rows // GROUP // STACK,),
        in_specs=[tile, tile, tile, block] + [whole(a) for a in arrays],
        out_specs=(block, *(whole(a) for a in outs)),
        out_shape=(jax.ShapeDtypeStruct(standard.shape, BF16), *outs),
        scratch_shapes=[
            pltpu.VMEM((2 * LANES, GROUP * width), BF16),
            pltpu.VMEM((2 * LANES, GROUP * width), BF16),
            pltpu.VMEM((rows // GROUP, LANES), F32),
            pltpu.VMEM((rows // GROUP, LANES), F32),
        ],
        compiler_params=pltpu.CompilerParams(vmem_limit_bytes=GRADIENT_LIMIT * MIB),
        cost_estimate=pl.CostEstimate(flops=16000 * MIB, bytes_accessed=22 * MIB, transcendentals=0),
        name="gradient_stage",
    )(weights, grad, small, standard, *arrays)


def per_device(
    atom_feats, atom_gain, atom_project, atom_merge, atom_up, token_counts, token_single, token_gain,
    token_project, token_merge, pair_state, pair_gain, bias_weight, atom_down, position_weight,
    position_cotangent,
):
    both = ("row", "col")
    rows, columns = lax.axis_size("row"), lax.axis_size("col")
    devices = rows * columns
    left = lax.ppermute(atom_feats, both, [(i, i + 1) for i in range(devices - 1)])
    right = lax.ppermute(atom_feats, both, [(i + 1, i) for i in range(devices - 1)])
    gain = pair_gain
    bias_turned = bias_weight.T
    groups = pair_state.shape[0] // GROUP
    cuts = (0, groups // 4, groups * 5 // 8, groups)
    pair_part = pair_forward(pair_state, gain, bias_turned, 0, cuts[1])
    hidden, state, packed, send = atom_stage(
        left, atom_feats, right, atom_gain, atom_project, atom_merge, atom_up,
        token_counts, token_single, token_gain, position_weight, position_cotangent, rows, pair_part[0],
    )
    pair_part = pair_forward(pair_state, gain, bias_turned, cuts[1], cuts[2] - cuts[1], pair_part, (send,))
    shared = lax.all_to_all(send, "row", 0, 0)
    shared = shared.reshape(columns, -1, shared.shape[-1])
    mixed = jnp.concatenate([shared, jnp.broadcast_to(packed[None], (columns,) + packed.shape)], axis=1)
    gathered = lax.all_to_all(mixed, "col", 0, 0)
    terms, standard = pair_forward(
        pair_state, gain, bias_turned, cuts[2], cuts[3] - cuts[2], pair_part, (mixed,)
    )
    weights, grad, small, payload = attend_stage(
        gathered, token_project, atom_down, token_merge, terms, columns
    )
    received = lax.all_to_all(payload, "col", 0, 0)
    pair_grad, positions, token_update = gradient_stage(
        weights, grad, small, standard, received, payload, gain, bias_turned,
        state, hidden, token_counts, token_merge, atom_down, position_weight,
    )
    return (positions, token_update, pair_grad)


def solution(mesh):
    placed = (
        P(("row", "col"), None), P(), P(), P(), P(), P(("row", "col"), None), P(("row", "col"), None), P(),
        P(), P(), P("row", "col", None), P(), P(), P(), P(), P(None, ("row", "col")),
    )
    return jax.shard_map(
        per_device,
        mesh=mesh,
        in_specs=placed,
        out_specs=(P(None, ("row", "col")), P(("row", "col"), None), P("row", "col", None)),
        check_vma=False,
    )
```

```python
import math

import jax
import jax.numpy as jnp
from jax import lax
from jax.experimental import pallas as pl
from jax.experimental.pallas import tpu as pltpu
from jax.sharding import PartitionSpec as P

ATOM_HEADS = 4
TOKEN_HEADS = 16
EPS = 1e-05
NEGATIVE = -1e30
LEFT, RIGHT = 48, 80
WINDOW = 32
KEYS = 128
LANES = 128
GROUP = 8
TERM_SLOTS = 8
KINDS = 3
ATTEND_STACK = 4
PAIR_STACK = 2
STACK = 4
F32 = jnp.float32
BF16 = jnp.bfloat16
NT = (((1,), (1,)), ((), ()))
TN = (((0,), (0,)), ((), ()))
MIB = 1 << 20
PAIR_LIMIT = 56
ATOM_LIMIT = 40
ATTEND_LIMIT = 46
GRADIENT_LIMIT = 32


def iota(shape, axis):
    return lax.broadcasted_iota(jnp.int32, shape, axis)


def dot(a, b):
    return jnp.dot(a, b, preferred_element_type=F32)


def dot_nt(a, b):
    return lax.dot_general(a, b, NT, preferred_element_type=F32)


def dot_tn(a, b):
    return lax.dot_general(a, b, TN, preferred_element_type=F32)


def split(value):
    high = value.astype(BF16)
    return high, (value - high.astype(F32)).astype(BF16)


def normalize(values, gain):
    center = values - jnp.mean(values, axis=-1, keepdims=True)
    spread = lax.rsqrt(jnp.mean(center * center, axis=-1, keepdims=True) + EPS)
    return center * spread * gain


def head_mask(rows, width, heads):
    size = width // heads
    head = iota((rows, width), 0) % heads
    column = iota((rows, width), 1)
    return ((column >= head * size) & (column < (head + 1) * size)).astype(F32)


def pair_kernel(x_ref, gain_ref, weight_ref, *rest):
    terms_ref, standard_ref, block_ref, ones_ref, normed_ref = rest[-5:]
    heads = weight_ref.shape[0]
    width = x_ref.shape[2]

    @pl.when(pl.program_id(0) == 0)
    def _():
        lane = iota((heads, LANES), 1)
        repeat = (lane % heads == iota((heads, LANES), 0)).astype(BF16)
        tiled = dot_tn(weight_ref[...], repeat)
        owner = iota((width, LANES), 1) // heads
        for i in range(GROUP):
            block_ref[i * width : (i + 1) * width, :] = jnp.where(owner == i, tiled, 0.0).astype(BF16)
        ones_ref[...] = jnp.full((width, width), 1.0 / width, BF16)

    gain = gain_ref[...][None, :]
    keys = x_ref.shape[1]
    owner = iota((keys, LANES), 1) // heads
    for q in range(PAIR_STACK):
        lanes = slice(q * LANES, (q + 1) * LANES)
        spread_all = jnp.zeros((keys, LANES), F32)
        for i in range(GROUP):
            x = x_ref[q * GROUP + i]
            center = x.astype(F32) - dot(x, ones_ref[...])
            spread = lax.rsqrt(jnp.sum(center * center, axis=1, keepdims=True) * (1.0 / width) + EPS)
            standard = center * spread
            standard_ref[q * GROUP + i] = standard.astype(BF16)
            normed_ref[q * keys : (q + 1) * keys, i * width : (i + 1) * width] = (standard * gain).astype(BF16)
            spread_all = jnp.where(owner == i, spread, spread_all)
        terms_ref[1, :, lanes] = spread_all
    bias = dot(normed_ref[...], block_ref[...])
    for q in range(PAIR_STACK):
        terms_ref[0, :, q * LANES : (q + 1) * LANES] = bias[q * keys : (q + 1) * keys]


def pair_forward(pair, gain, weight, first, count, previous=(), after=()):
    rows, keys, width = pair.shape
    heads = weight.shape[0]
    lanes = rows * heads
    outs = (
        jax.ShapeDtypeStruct((TERM_SLOTS, keys, lanes), F32),
        jax.ShapeDtypeStruct(pair.shape, BF16),
    )
    before = tuple(previous)
    others = before + tuple(after)
    return pl.pallas_call(
        pair_kernel,
        grid=(count // PAIR_STACK,),
        in_specs=[
            pl.BlockSpec((PAIR_STACK * GROUP, keys, width), lambda g: (g + first // PAIR_STACK, 0, 0)),
            whole(gain),
            whole(weight),
        ]
        + [pl.BlockSpec(memory_space=pl.ANY)] * len(others),
        out_specs=(
            pl.BlockSpec((2, keys, PAIR_STACK * LANES), lambda g: (0, 0, g + first // PAIR_STACK)),
            pl.BlockSpec((PAIR_STACK * GROUP, keys, width), lambda g: (g + first // PAIR_STACK, 0, 0)),
        ),
        out_shape=outs,
        scratch_shapes=[
            pltpu.VMEM((GROUP * width, LANES), BF16),
            pltpu.VMEM((width, width), BF16),
            pltpu.VMEM((PAIR_STACK * keys, GROUP * width), BF16),
        ],
        input_output_aliases={3 + i: i for i in range(len(before))},
        compiler_params=pltpu.CompilerParams(vmem_limit_bytes=PAIR_LIMIT * MIB),
        cost_estimate=pl.CostEstimate(
            flops=count * GROUP * keys * width * 5000, bytes_accessed=count * GROUP * keys * width * 5, transcendentals=0
        ),
        name="pair_forward",
    )(pair, gain, weight, *others)


def atom_kernel(
    left_ref, own_ref, right_ref, gain_ref, project_ref, merge_ref, up_ref,
    counts_ref, single_ref, token_gain_ref, weight_ref, cotangent_ref, _,
    hidden_ref, state_ref, packed_ref, send_ref, key_ref, value_ref, query_ref, attended_ref,
):
    atoms, width = own_ref.shape
    tokens = single_ref.shape[0]
    rows, columns = lax.axis_size("row"), lax.axis_size("col")
    first = (lax.axis_index("row") * columns + lax.axis_index("col")) * atoms
    feats = jnp.concatenate(
        [left_ref[atoms - LEFT :, :], own_ref[...], right_ref[:RIGHT, :]], axis=0
    )
    normed = normalize(feats.astype(F32), gain_ref[...][None, :]).astype(BF16)
    projected = dot(normed, project_ref[...]).astype(BF16)
    query_ref[...] = projected[LEFT : LEFT + atoms, :width]
    key_ref[...] = projected[:, width : 2 * width]
    value_ref[...] = projected[:, 2 * width :]
    size = width // ATOM_HEADS
    stacked = ATOM_HEADS * WINDOW
    lane_head = iota((stacked, width), 1) // size
    row_head = iota((stacked, width), 0) // WINDOW
    mask = lane_head == row_head
    key_index = iota((stacked, KEYS), 1)
    total = rows * columns * atoms
    for b in range(atoms // WINDOW):
        at = b * WINDOW
        queries = jnp.concatenate([query_ref[at : at + WINDOW, :]] * ATOM_HEADS, axis=0)
        queries = jnp.where(mask, queries.astype(F32), 0.0).astype(BF16)
        scores = dot_nt(queries, key_ref[at : at + KEYS, :]) / math.sqrt(size)
        position = first - LEFT + at + key_index
        scores = jnp.where((position >= 0) & (position < total), scores, NEGATIVE)
        weights = jnp.exp(scores - jnp.max(scores, axis=1, keepdims=True))
        row_total = jnp.sum(weights, axis=1, keepdims=True)
        mixture = dot(weights.astype(BF16), value_ref[at : at + KEYS, :]) / row_total
        mixture = jnp.where(mask, mixture, 0.0)
        joined = mixture[:WINDOW]
        for h in range(1, ATOM_HEADS):
            joined = joined + mixture[h * WINDOW : (h + 1) * WINDOW]
        attended_ref[at : at + WINDOW, :] = joined.astype(BF16)
    hidden = (own_ref[...].astype(F32) + dot(attended_ref[...], merge_ref[...])).astype(BF16)
    hidden_ref[...] = hidden
    lifted = jnp.maximum(dot(hidden, up_ref[...]), 0.0).astype(BF16)
    counts_row = counts_ref[...].astype(F32)
    square = jnp.broadcast_to(counts_row, (tokens, tokens))
    above = iota((tokens, tokens), 0)
    below = iota((tokens, tokens), 1)
    counts_col = jnp.sum(jnp.where(above == below, square, 0.0), axis=1, keepdims=True)
    ends = jnp.sum(jnp.where(below <= above, square, 0.0), axis=1, keepdims=True)
    atom = iota((tokens, atoms), 1).astype(F32)
    member = ((atom < ends) & (atom >= ends - counts_col)).astype(F32).astype(BF16)
    state = dot(member, lifted) / counts_col + single_ref[...].astype(F32)
    state_ref[...] = state
    token_normed = normalize(state, token_gain_ref[...][None, :]).astype(BF16)
    turned = jnp.transpose(
        jnp.concatenate([cotangent_ref[...], jnp.zeros((LANES - 3, atoms), F32)], axis=0)
    )
    position_weight = weight_ref[...].astype(F32)
    grad_hidden = turned[:, 0:1] * position_weight[0:1, :]
    for k in range(1, 3):
        grad_hidden = grad_hidden + turned[:, k : k + 1] * position_weight[k : k + 1, :]
    grad_tokens = dot(member, grad_hidden.astype(BF16)).astype(BF16)
    tiles = [token_normed[:, t * LANES : (t + 1) * LANES] for t in range(token_normed.shape[1] // LANES)]
    block = jnp.concatenate(tiles, axis=0)
    packed_ref[...] = jnp.concatenate([block, grad_tokens], axis=0)
    for c in range(send_ref.shape[0]):
        send_ref[c] = block


def whole(array):
    zeros = (0,) * array.ndim
    return pl.BlockSpec(array.shape, lambda *_: zeros)


def atom_stage(left, own, right, gain, project, merge, up, counts, single, token_gain, weight, cotangent, copies, after):
    atoms, width = own.shape
    tokens, token_width = single.shape
    arrays = (left, own, right, gain, project, merge, up, counts, single, token_gain, weight, cotangent)
    outs = (
        jax.ShapeDtypeStruct((atoms, width), BF16),
        jax.ShapeDtypeStruct((tokens, token_width), F32),
        jax.ShapeDtypeStruct((tokens * token_width // LANES + tokens, LANES), BF16),
        jax.ShapeDtypeStruct((copies, tokens * token_width // LANES, LANES), BF16),
    )
    return pl.pallas_call(
        atom_kernel,
        grid=(1,),
        in_specs=[whole(a) for a in arrays]
        + [pl.BlockSpec(memory_space=pl.ANY)],
        out_specs=tuple(whole(a) for a in outs),
        out_shape=outs,
        scratch_shapes=[
            pltpu.VMEM((LEFT + atoms + RIGHT, width), BF16),
            pltpu.VMEM((LEFT + atoms + RIGHT, width), BF16),
            pltpu.VMEM((atoms, width), BF16),
            pltpu.VMEM((atoms, width), BF16),
        ],
        compiler_params=pltpu.CompilerParams(vmem_limit_bytes=ATOM_LIMIT * MIB),
        cost_estimate=pl.CostEstimate(flops=400 * MIB, bytes_accessed=2 * MIB, transcendentals=0),
        name="atom_stage",
    )(*arrays, after)


def attend_kernel(
    gathered_ref, down_ref, project_hbm, merge_hbm, terms_hbm,
    weight_ref, grad_ref, small_ref, send_ref,
    query_ref, mix_ref, key_ref, value_ref, stat_ref, project_ref, merge_ref, terms_ref,
    weight_semaphores, semaphores,
):
    step = pl.program_id(0)
    owners = send_ref.shape[0]
    steps = owners // ATTEND_STACK
    width = project_ref.shape[1]
    heads = TOKEN_HEADS
    chunk = weight_ref.shape[1]
    per = chunk // LANES
    stat_rows = steps * per
    part_rows = query_ref.shape[0] // owners
    part_lanes = chunk // ATTEND_STACK

    def terms_copy(at):
        lanes = pl.ds(pl.multiple_of(at * chunk, chunk), chunk)
        return pltpu.make_async_copy(terms_hbm.at[0:2, :, lanes], terms_ref.at[:, :, lanes], semaphores.at[at])

    @pl.when(step == 0)
    def _():
        thirds = [
            pltpu.make_async_copy(
                project_hbm.at[:, k * width : (k + 1) * width], project_ref.at[k], weight_semaphores.at[k]
            )
            for k in range(3)
        ]
        merge = pltpu.make_async_copy(merge_hbm, merge_ref, weight_semaphores.at[3])
        for copy in (*thirds, merge, terms_copy(0), terms_copy(1)):
            copy.start()
        tiles = width // LANES
        own = gathered_ref.shape[1] // (KINDS * tiles + 1)

        def tile(index):
            return gathered_ref[:, index * own : (index + 1) * own, :].reshape(-1, LANES)

        blocks = [
            jnp.concatenate([tile(k * tiles + t) for t in range(tiles)], axis=1) for k in range(KINDS)
        ]
        rows = jnp.concatenate(blocks[:-1], axis=0)
        update = dot_nt(tile(KINDS * tiles), down_ref[...]).astype(BF16)
        thirds[0].wait()
        query_ref[...] = dot(blocks[-1], project_ref[0]).astype(BF16)
        thirds[1].wait()
        key_ref[...] = dot(rows, project_ref[1]).astype(BF16)
        thirds[2].wait()
        value_ref[...] = dot(rows, project_ref[2]).astype(BF16)
        merge.wait()
        mix_ref[...] = dot_nt(update, merge_ref[...]).astype(BF16)

    @pl.when(step < steps - 2)
    def _():
        terms_copy(step + 2).start()

    terms_copy(step).wait()
    mask = head_mask(heads, width, heads)

    def expanded(ref, at):
        own = pl.ds(pl.multiple_of(at * part_rows, part_rows), part_rows)
        spread_out = ref[own, :].astype(F32)[:, None, :] * mask[None]
        return spread_out.reshape(part_rows * heads, width).astype(BF16)

    values = value_ref[...]
    all_rounded = []
    for sub in range(ATTEND_STACK):
        at = step * ATTEND_STACK + sub
        inside = slice(sub * part_lanes, (sub + 1) * part_lanes)
        lanes = pl.ds(pl.multiple_of(at * part_lanes, part_lanes), part_lanes)
        bias = terms_ref[0, :, lanes]
        scores = dot_nt(key_ref[...], expanded(query_ref, at)) / math.sqrt(width // heads) + bias
        grad_probs = dot_nt(values, expanded(mix_ref, at))
        row_max = jnp.max(scores, axis=0, keepdims=True).astype(BF16).astype(F32)
        weights = jnp.exp(scores - row_max)
        row_total = jnp.sum(weights, axis=0, keepdims=True)
        rounded = weights.astype(BF16)
        all_rounded.append(rounded)
        inner = jnp.sum(rounded.astype(F32) * grad_probs, axis=0, keepdims=True)
        weight_ref[:, inside] = (weights * terms_ref[1, :, lanes]).astype(BF16)
        grad_ref[:, inside] = grad_probs
        small_ref[:, inside] = (bias * (1.0 / LANES)).astype(BF16)
        for k, stat in enumerate((row_max, row_total, inner)):
            for p in range(part_lanes // LANES):
                row = k * stat_rows + at * (part_lanes // LANES) + p
                stat_ref[pl.ds(row, 1), :] = stat[:, p * LANES : (p + 1) * LANES]
    mixture = dot_tn(jnp.concatenate(all_rounded, axis=1), values).reshape(-1, heads, width) * mask[None]
    part = jnp.sum(mixture, axis=1).astype(BF16)
    for sub in range(ATTEND_STACK):
        for t in range(width // LANES):
            low = 5 * stat_rows + t * part_rows
            send_ref[step * ATTEND_STACK + sub, low : low + part_rows, :] = part[
                sub * part_rows : (sub + 1) * part_rows, t * LANES : (t + 1) * LANES
            ]

    @pl.when(step == steps - 1)
    def _():
        pieces = [stat_ref[:stat_rows, :].astype(BF16)]
        for k in (1, 2):
            pieces.extend(split(stat_ref[k * stat_rows : (k + 1) * stat_rows, :]))
        stats = jnp.concatenate(pieces, axis=0)
        for c in range(owners):
            send_ref[c, : 5 * stat_rows, :] = stats


def attend_stage(gathered, project, down, merge, terms, owners):
    _, keys, lanes = terms.shape
    width = project.shape[0]
    count = gathered.shape[0] * gathered.shape[1] // (KINDS * (width // LANES) + 1)
    rows = count // owners
    steps = owners // ATTEND_STACK
    chunk = lanes // steps
    stat_rows = lanes // LANES
    payload = jax.ShapeDtypeStruct((owners, 5 * stat_rows + rows * width // LANES, LANES), BF16)
    tile = pl.BlockSpec((keys, chunk), lambda g: (0, g))
    arrays = (gathered, down)
    return pl.pallas_call(
        attend_kernel,
        grid=(steps,),
        in_specs=[whole(a) for a in arrays] + [pl.BlockSpec(memory_space=pl.ANY)] * 3,
        out_specs=(tile, tile, tile, whole(payload)),
        out_shape=(
            jax.ShapeDtypeStruct((keys, lanes), BF16),
            jax.ShapeDtypeStruct((keys, lanes), F32),
            jax.ShapeDtypeStruct((keys, lanes), BF16),
            payload,
        ),
        scratch_shapes=[
            pltpu.VMEM((count, width), BF16),
            pltpu.VMEM((count, width), BF16),
            pltpu.VMEM((keys, width), BF16),
            pltpu.VMEM((keys, width), BF16),
            pltpu.VMEM((3 * stat_rows, LANES), F32),
            pltpu.VMEM((3, width, width), BF16),
            pltpu.VMEM((width, width), BF16),
            pltpu.VMEM((2, keys, lanes), F32),
            pltpu.SemaphoreType.DMA((4,)),
            pltpu.SemaphoreType.DMA((steps,)),
        ],
        compiler_params=pltpu.CompilerParams(vmem_limit_bytes=ATTEND_LIMIT * MIB),
        cost_estimate=pl.CostEstimate(flops=8000 * MIB, bytes_accessed=12 * MIB, transcendentals=0),
        name="attend_stage",
    )(*arrays, project, merge, terms)


def combined(received_ref, rows):
    parts = received_ref.shape[0]

    def stat(part, index):
        return received_ref[part, index * rows : (index + 1) * rows, :].astype(F32)

    maxima = [stat(s, 0) for s in range(parts)]
    top = maxima[0]
    for s in range(1, parts):
        top = jnp.maximum(top, maxima[s])
    scales = [jnp.exp(value - top) for value in maxima]
    total = jnp.zeros_like(top)
    inner = jnp.zeros_like(top)
    for s in range(parts):
        total = total + scales[s] * (stat(s, 1) + stat(s, 2))
        inner = inner + scales[s] * (stat(s, 3) + stat(s, 4))
    return top, scales, total, inner


def update_tokens(
    received_ref, state_ref, hidden_ref, counts_ref, merge_ref, down_ref, weight_ref, positions_ref, update_ref,
    scales, total,
):
    column = lax.axis_index("col")
    tokens, width = state_ref.shape
    heads = TOKEN_HEADS
    parts = received_ref.shape[0]
    stat_rows = (received_ref.shape[1] - tokens * width // LANES) // 5
    halves = tokens // GROUP
    sub = iota((tokens, LANES), 0)
    mine = iota((tokens, LANES), 1) // heads == sub % GROUP
    stat_row = iota((stat_rows, LANES), 0)
    rows = []
    for s in range(parts):
        scale = scales[s] / total
        picked = jnp.zeros((tokens, LANES), F32)
        for p in range(halves):
            one = jnp.sum(jnp.where(stat_row == column * halves + p, scale, 0.0), axis=0, keepdims=True)
            picked = jnp.where(sub // GROUP == p, one, picked)
        rows.append(jnp.where(mine, picked, 0.0))
    stacked = jnp.concatenate(rows, axis=0)
    spread_out = head_mask(LANES, width, heads).astype(BF16)
    high, low = split(stacked)
    rest = stacked - high.astype(F32) - low.astype(F32)
    scale = dot(high, spread_out) + dot(low, spread_out) + dot(rest.astype(BF16), spread_out)
    pieces = []
    for t in range(width // LANES):
        at = 5 * stat_rows + t * tokens
        piece = jnp.zeros((tokens, LANES), F32)
        for s in range(parts):
            factor = scale[s * tokens : (s + 1) * tokens, t * LANES : (t + 1) * LANES]
            piece = piece + factor * received_ref[s, at : at + tokens, :].astype(F32)
        pieces.append(piece.astype(BF16))
    attention = jnp.concatenate(pieces, axis=1)
    update = (state_ref[...] + dot(attention, merge_ref[...])).astype(BF16)
    update_ref[...] = update
    lowered = dot(update, down_ref[...]).astype(BF16)
    atoms = hidden_ref.shape[0]
    counts_row = counts_ref[...].astype(F32)
    square = jnp.broadcast_to(counts_row, (tokens, tokens))
    above = iota((tokens, tokens), 0)
    below = iota((tokens, tokens), 1)
    counts_col = jnp.sum(jnp.where(above == below, square, 0.0), axis=1, keepdims=True)
    ends = jnp.sum(jnp.where(below <= above, square, 0.0), axis=1, keepdims=True)
    atom = iota((tokens, atoms), 1).astype(F32)
    member = ((atom < ends) & (atom >= ends - counts_col)).astype(F32).astype(BF16)
    hidden_next = (hidden_ref[...].astype(F32) + dot_tn(member, lowered)).astype(BF16)
    positions_ref[...] = dot_nt(weight_ref[...], hidden_next)


def gradient_kernel(
    weight_ref, grad_ref, small_ref, standard_ref, received_ref, own_ref, gain_ref, bias_weight_ref,
    state_ref, hidden_ref, counts_ref, merge_ref, down_ref, position_ref,
    out_hbm, positions_ref, update_ref, block_ref, ones_ref, factor_ref, inner_ref, slots_ref, semaphores,
):
    step = pl.program_id(0)
    heads, width = bias_weight_ref.shape
    rows = factor_ref.shape[0]

    @pl.when(step == 0)
    def _():
        lane = iota((heads, LANES), 1)
        repeat = (lane % heads == iota((heads, LANES), 0)).astype(BF16)
        tiled = dot_tn(repeat, bias_weight_ref[...]) * gain_ref[...][None, :]
        tiled = tiled - jnp.mean(tiled, axis=1, keepdims=True)
        high, low = split(tiled)
        owner = iota((LANES, width), 0) // heads
        for i in range(GROUP):
            mine = owner == i
            at = slice(i * width, (i + 1) * width)
            block_ref[:LANES, at] = jnp.where(mine, high.astype(F32), 0.0).astype(BF16)
            block_ref[LANES:, at] = jnp.where(mine, low.astype(F32), 0.0).astype(BF16)
            ones = jnp.where(mine, 1.0, 0.0).astype(BF16)
            ones_ref[:LANES, at] = ones
            ones_ref[LANES:, at] = ones
        top, _, total, inner = combined(received_ref, rows)
        factor_ref[...] = jnp.exp(own_ref[0, :rows, :].astype(F32) - top) / total
        inner_ref[...] = inner / total

    steps = pl.num_programs(0)
    slot = step % 2
    count = slots_ref.shape[1]

    def out_copy(at):
        return pltpu.make_async_copy(
            slots_ref.at[at % 2], out_hbm.at[pl.ds(at * count, count)], semaphores.at[at % 2]
        )

    @pl.when(step >= 2)
    def _():
        out_copy(step - 2).wait()

    keys = weight_ref.shape[0]
    lefts, rights = [], []
    for q in range(STACK):
        lanes = slice(q * LANES, (q + 1) * LANES)
        factor = factor_ref[pl.ds(step * STACK + q, 1), :]
        inner = inner_ref[pl.ds(step * STACK + q, 1), :]
        grad = weight_ref[:, lanes].astype(F32) * factor * (grad_ref[:, lanes] - inner)
        rounded = grad.astype(BF16)
        lefts.append(jnp.concatenate([rounded, rounded], axis=1))
        rights.append(jnp.concatenate(split(grad * small_ref[:, lanes].astype(F32)), axis=1))
    left = jnp.concatenate(lefts, axis=0)
    right = jnp.concatenate(rights, axis=0)
    for i in range(0, GROUP, 2):
        at = slice(i * width, (i + 2) * width)
        direct = dot(left, block_ref[:, at])
        along = dot(right, ones_ref[:, at])
        for q in range(STACK):
            for k in range(2):
                part = (slice(q * keys, (q + 1) * keys), slice(k * width, (k + 1) * width))
                r = q * GROUP + i + k
                slots_ref[slot, r] = (direct[part] - standard_ref[r].astype(F32) * along[part]).astype(BF16)

    out_copy(step).start()

    @pl.when(step == steps - 1)
    def _():
        _, scales, total, _ = combined(received_ref, rows)
        update_tokens(
            received_ref, state_ref, hidden_ref, counts_ref, merge_ref, down_ref, position_ref,
            positions_ref, update_ref, scales, total,
        )
        out_copy(step - 1).wait()
        out_copy(step).wait()


def gradient_stage(weights, grad, small, standard, received, own, gain, bias_weight, state, hidden, counts, merge, down, weight):
    rows, keys, width = standard.shape
    arrays = (received, own, gain, bias_weight, state, hidden, counts, merge, down, weight)
    outs = (
        jax.ShapeDtypeStruct((weight.shape[0], hidden.shape[0]), F32),
        jax.ShapeDtypeStruct(state.shape, BF16),
    )
    tile = pl.BlockSpec((keys, STACK * LANES), lambda g: (0, g))
    block = pl.BlockSpec((STACK * GROUP, keys, width), lambda g: (g, 0, 0))
    return pl.pallas_call(
        gradient_kernel,
        grid=(rows // GROUP // STACK,),
        in_specs=[tile, tile, tile, block] + [whole(a) for a in arrays],
        out_specs=(pl.BlockSpec(memory_space=pl.ANY), *(whole(a) for a in outs)),
        out_shape=(jax.ShapeDtypeStruct(standard.shape, BF16), *outs),
        scratch_shapes=[
            pltpu.VMEM((2 * LANES, GROUP * width), BF16),
            pltpu.VMEM((2 * LANES, GROUP * width), BF16),
            pltpu.VMEM((rows // GROUP, LANES), F32),
            pltpu.VMEM((rows // GROUP, LANES), F32),
            pltpu.VMEM((2, STACK * GROUP, keys, width), BF16),
            pltpu.SemaphoreType.DMA((2,)),
        ],
        compiler_params=pltpu.CompilerParams(vmem_limit_bytes=GRADIENT_LIMIT * MIB),
        cost_estimate=pl.CostEstimate(flops=16000 * MIB, bytes_accessed=22 * MIB, transcendentals=0),
        name="gradient_stage",
    )(weights, grad, small, standard, *arrays)


def per_device(
    atom_feats, atom_gain, atom_project, atom_merge, atom_up, token_counts, token_single, token_gain,
    token_project, token_merge, pair_state, pair_gain, bias_weight, atom_down, position_weight,
    position_cotangent,
):
    both = ("row", "col")
    rows, columns = lax.axis_size("row"), lax.axis_size("col")
    devices = rows * columns
    left = lax.ppermute(atom_feats, both, [(i, i + 1) for i in range(devices - 1)])
    right = lax.ppermute(atom_feats, both, [(i + 1, i) for i in range(devices - 1)])
    gain = pair_gain
    bias_turned = bias_weight.T
    groups = pair_state.shape[0] // GROUP
    cuts = (0, groups // 4, groups * 5 // 8, groups)
    pair_part = pair_forward(pair_state, gain, bias_turned, 0, cuts[1])
    hidden, state, packed, send = atom_stage(
        left, atom_feats, right, atom_gain, atom_project, atom_merge, atom_up,
        token_counts, token_single, token_gain, position_weight, position_cotangent, rows, pair_part[0],
    )
    pair_part = pair_forward(pair_state, gain, bias_turned, cuts[1], cuts[2] - cuts[1], pair_part, (send,))
    shared = lax.all_to_all(send, "row", 0, 0)
    shared = shared.reshape(columns, -1, shared.shape[-1])
    mixed = jnp.concatenate([shared, jnp.broadcast_to(packed[None], (columns,) + packed.shape)], axis=1)
    gathered = lax.all_to_all(mixed, "col", 0, 0)
    terms, standard = pair_forward(
        pair_state, gain, bias_turned, cuts[2], cuts[3] - cuts[2], pair_part, (mixed,)
    )
    weights, grad, small, payload = attend_stage(
        gathered, token_project, atom_down, token_merge, terms, columns
    )
    received = lax.all_to_all(payload, "col", 0, 0)
    pair_grad, positions, token_update = gradient_stage(
        weights, grad, small, standard, received, payload, gain, bias_turned,
        state, hidden, token_counts, token_merge, atom_down, position_weight,
    )
    return (positions, token_update, pair_grad)


def solution(mesh):
    placed = (
        P(("row", "col"), None), P(), P(), P(), P(), P(("row", "col"), None), P(("row", "col"), None), P(),
        P(), P(), P("row", "col", None), P(), P(), P(), P(), P(None, ("row", "col")),
    )
    return jax.shard_map(
        per_device,
        mesh=mesh,
        in_specs=placed,
        out_specs=(P(None, ("row", "col")), P(("row", "col"), None), P("row", "col", None)),
        check_vma=False,
    )
```

```python
import jax
import jax.numpy as jnp
from jax import lax
from jax.experimental import pallas as pl
from jax.experimental.pallas import tpu as pltpu
from jax.sharding import PartitionSpec as P

ATOM_HEADS = 4
TOKEN_HEADS = 16
EPS = 1e-05
NEGATIVE = -1e30
LEFT, RIGHT = 48, 80
WINDOW = 32
KEYS = 128
LANES = 128
GROUP = 8
TERM_SLOTS = 8
KINDS = 3
ATTEND_STACK = 4
PAIR_STACK = 2
STACK = 4
F32 = jnp.float32
BF16 = jnp.bfloat16
NT = (((1,), (1,)), ((), ()))
TN = (((0,), (0,)), ((), ()))
MIB = 1 << 20
PAIR_LIMIT = 56
ATOM_LIMIT = 40
ATTEND_LIMIT = 46
GRADIENT_LIMIT = 32


def iota(shape, axis):
    return lax.broadcasted_iota(jnp.int32, shape, axis)


def dot(a, b):
    return jnp.dot(a, b, preferred_element_type=F32)


def dot_nt(a, b):
    return lax.dot_general(a, b, NT, preferred_element_type=F32)


def dot_tn(a, b):
    return lax.dot_general(a, b, TN, preferred_element_type=F32)


def split(value):
    high = value.astype(BF16)
    return high, (value - high.astype(F32)).astype(BF16)


def normalize(values, gain):
    center = values - jnp.mean(values, axis=-1, keepdims=True)
    spread = lax.rsqrt(jnp.mean(center * center, axis=-1, keepdims=True) + EPS)
    return center * spread * gain


def head_mask(rows, width, heads):
    size = width // heads
    head = iota((rows, width), 0) % heads
    column = iota((rows, width), 1)
    return ((column >= head * size) & (column < (head + 1) * size)).astype(F32)


def pair_kernel(x_ref, gain_ref, weight_ref, *rest):
    terms_ref, standard_ref, block_ref, ones_ref, normed_ref = rest[-5:]
    heads = weight_ref.shape[0]
    width = x_ref.shape[2]

    @pl.when(pl.program_id(0) == 0)
    def _():
        lane = iota((heads, LANES), 1)
        repeat = (lane % heads == iota((heads, LANES), 0)).astype(BF16)
        tiled = dot_tn(weight_ref[...], repeat)
        owner = iota((width, LANES), 1) // heads
        for i in range(GROUP):
            block_ref[i * width : (i + 1) * width, :] = jnp.where(owner == i, tiled, 0.0).astype(BF16)
        ones_ref[...] = jnp.full((width, width), 1.0 / width, BF16)

    gain = gain_ref[...][None, :]
    keys = x_ref.shape[1]
    owner = iota((keys, LANES), 1) // heads
    for q in range(PAIR_STACK):
        lanes = slice(q * LANES, (q + 1) * LANES)
        spread_all = jnp.zeros((keys, LANES), F32)
        for i in range(GROUP):
            x = x_ref[q * GROUP + i]
            center = x.astype(F32) - dot(x, ones_ref[...])
            spread = lax.rsqrt(jnp.sum(center * center, axis=1, keepdims=True) * (1.0 / width) + EPS)
            standard = center * spread
            standard_ref[q * GROUP + i] = standard.astype(BF16)
            normed_ref[q * keys : (q + 1) * keys, i * width : (i + 1) * width] = (standard * gain).astype(BF16)
            spread_all = jnp.where(owner == i, spread, spread_all)
        terms_ref[1, :, lanes] = spread_all
    bias = dot(normed_ref[...], block_ref[...])
    for q in range(PAIR_STACK):
        terms_ref[0, :, q * LANES : (q + 1) * LANES] = bias[q * keys : (q + 1) * keys]


def pair_forward(pair, gain, weight, first, count, previous=(), after=()):
    rows, keys, width = pair.shape
    heads = weight.shape[0]
    lanes = rows * heads
    outs = (
        jax.ShapeDtypeStruct((TERM_SLOTS, keys, lanes), F32),
        jax.ShapeDtypeStruct(pair.shape, BF16),
    )
    before = tuple(previous)
    others = before + tuple(after)
    return pl.pallas_call(
        pair_kernel,
        grid=(count // PAIR_STACK,),
        in_specs=[
            pl.BlockSpec((PAIR_STACK * GROUP, keys, width), lambda g: (g + first // PAIR_STACK, 0, 0)),
            whole(gain),
            whole(weight),
        ]
        + [pl.BlockSpec(memory_space=pl.ANY)] * len(others),
        out_specs=(
            pl.BlockSpec((2, keys, PAIR_STACK * LANES), lambda g: (0, 0, g + first // PAIR_STACK)),
            pl.BlockSpec((PAIR_STACK * GROUP, keys, width), lambda g: (g + first // PAIR_STACK, 0, 0)),
        ),
        out_shape=outs,
        scratch_shapes=[
            pltpu.VMEM((GROUP * width, LANES), BF16),
            pltpu.VMEM((width, width), BF16),
            pltpu.VMEM((PAIR_STACK * keys, GROUP * width), BF16),
        ],
        input_output_aliases={3 + i: i for i in range(len(before))},
        compiler_params=pltpu.CompilerParams(vmem_limit_bytes=PAIR_LIMIT * MIB),
        cost_estimate=pl.CostEstimate(
            flops=count * GROUP * keys * width * 5000, bytes_accessed=count * GROUP * keys * width * 5, transcendentals=0
        ),
        name="pair_forward",
    )(pair, gain, weight, *others)


def atom_kernel(
    left_ref, own_ref, right_ref, gain_ref, project_ref, merge_ref, up_ref,
    counts_ref, single_ref, token_gain_ref, weight_ref, cotangent_ref, _,
    hidden_ref, state_ref, packed_ref, send_ref, key_ref, value_ref, query_ref, attended_ref,
):
    atoms, width = own_ref.shape
    tokens = single_ref.shape[0]
    rows, columns = lax.axis_size("row"), lax.axis_size("col")
    first = (lax.axis_index("row") * columns + lax.axis_index("col")) * atoms
    feats = jnp.concatenate(
        [left_ref[atoms - LEFT :, :], own_ref[...], right_ref[:RIGHT, :]], axis=0
    )
    normed = normalize(feats.astype(F32), gain_ref[...][None, :]).astype(BF16)
    projected = dot(normed, project_ref[...]).astype(BF16)
    query_ref[...] = projected[LEFT : LEFT + atoms, :width]
    key_ref[...] = projected[:, width : 2 * width]
    value_ref[...] = projected[:, 2 * width :]
    size = width // ATOM_HEADS
    stacked = ATOM_HEADS * WINDOW
    lane_head = iota((stacked, width), 1) // size
    row_head = iota((stacked, width), 0) // WINDOW
    mask = lane_head == row_head
    key_index = iota((stacked, KEYS), 1)
    total = rows * columns * atoms
    for b in range(atoms // WINDOW):
        at = b * WINDOW
        queries = jnp.concatenate([query_ref[at : at + WINDOW, :]] * ATOM_HEADS, axis=0)
        queries = jnp.where(mask, queries.astype(F32), 0.0).astype(BF16)
        scores = dot_nt(queries, key_ref[at : at + KEYS, :]) * size**-0.5
        position = first - LEFT + at + key_index
        scores = jnp.where((position >= 0) & (position < total), scores, NEGATIVE)
        weights = jnp.exp(scores - jnp.max(scores, axis=1, keepdims=True))
        row_total = jnp.sum(weights, axis=1, keepdims=True)
        mixture = dot(weights.astype(BF16), value_ref[at : at + KEYS, :]) / row_total
        mixture = jnp.where(mask, mixture, 0.0)
        joined = mixture[:WINDOW]
        for h in range(1, ATOM_HEADS):
            joined = joined + mixture[h * WINDOW : (h + 1) * WINDOW]
        attended_ref[at : at + WINDOW, :] = joined.astype(BF16)
    hidden = (own_ref[...].astype(F32) + dot(attended_ref[...], merge_ref[...])).astype(BF16)
    hidden_ref[...] = hidden
    lifted = jnp.maximum(dot(hidden, up_ref[...]), 0.0).astype(BF16)
    counts_row = counts_ref[...].astype(F32)
    square = jnp.broadcast_to(counts_row, (tokens, tokens))
    above = iota((tokens, tokens), 0)
    below = iota((tokens, tokens), 1)
    counts_col = jnp.sum(jnp.where(above == below, square, 0.0), axis=1, keepdims=True)
    ends = jnp.sum(jnp.where(below <= above, square, 0.0), axis=1, keepdims=True)
    atom = iota((tokens, atoms), 1).astype(F32)
    member = ((atom < ends) & (atom >= ends - counts_col)).astype(F32).astype(BF16)
    state = dot(member, lifted) / counts_col + single_ref[...].astype(F32)
    state_ref[...] = state
    token_normed = normalize(state, token_gain_ref[...][None, :]).astype(BF16)
    turned = jnp.transpose(
        jnp.concatenate([cotangent_ref[...], jnp.zeros((LANES - 3, atoms), F32)], axis=0)
    )
    position_weight = weight_ref[...].astype(F32)
    grad_hidden = turned[:, 0:1] * position_weight[0:1, :]
    for k in range(1, 3):
        grad_hidden = grad_hidden + turned[:, k : k + 1] * position_weight[k : k + 1, :]
    grad_tokens = dot(member, grad_hidden.astype(BF16)).astype(BF16)
    tiles = [token_normed[:, t * LANES : (t + 1) * LANES] for t in range(token_normed.shape[1] // LANES)]
    block = jnp.concatenate(tiles, axis=0)
    packed_ref[...] = jnp.concatenate([block, grad_tokens], axis=0)
    for c in range(send_ref.shape[0]):
        send_ref[c] = block


def whole(array):
    zeros = (0,) * array.ndim
    return pl.BlockSpec(array.shape, lambda *_: zeros)


def atom_stage(left, own, right, gain, project, merge, up, counts, single, token_gain, weight, cotangent, copies, after):
    atoms, width = own.shape
    tokens, token_width = single.shape
    arrays = (left, own, right, gain, project, merge, up, counts, single, token_gain, weight, cotangent)
    outs = (
        jax.ShapeDtypeStruct((atoms, width), BF16),
        jax.ShapeDtypeStruct((tokens, token_width), F32),
        jax.ShapeDtypeStruct((tokens * token_width // LANES + tokens, LANES), BF16),
        jax.ShapeDtypeStruct((copies, tokens * token_width // LANES, LANES), BF16),
    )
    return pl.pallas_call(
        atom_kernel,
        grid=(1,),
        in_specs=[whole(a) for a in arrays]
        + [pl.BlockSpec(memory_space=pl.ANY)],
        out_specs=tuple(whole(a) for a in outs),
        out_shape=outs,
        scratch_shapes=[
            pltpu.VMEM((LEFT + atoms + RIGHT, width), BF16),
            pltpu.VMEM((LEFT + atoms + RIGHT, width), BF16),
            pltpu.VMEM((atoms, width), BF16),
            pltpu.VMEM((atoms, width), BF16),
        ],
        compiler_params=pltpu.CompilerParams(vmem_limit_bytes=ATOM_LIMIT * MIB),
        cost_estimate=pl.CostEstimate(flops=400 * MIB, bytes_accessed=2 * MIB, transcendentals=0),
        name="atom_stage",
    )(*arrays, after)


def attend_kernel(
    gathered_ref, down_ref, project_hbm, merge_hbm, terms_hbm,
    weight_ref, grad_ref, small_ref, send_ref,
    query_ref, mix_ref, key_ref, value_ref, stat_ref, project_ref, merge_ref, terms_ref,
    weight_semaphores, semaphores,
):
    step = pl.program_id(0)
    owners = send_ref.shape[0]
    steps = owners // ATTEND_STACK
    width = project_ref.shape[1]
    heads = TOKEN_HEADS
    chunk = weight_ref.shape[1]
    per = chunk // LANES
    stat_rows = steps * per
    part_rows = query_ref.shape[0] // owners
    part_lanes = chunk // ATTEND_STACK

    def terms_copy(at):
        lanes = pl.ds(pl.multiple_of(at * chunk, chunk), chunk)
        return pltpu.make_async_copy(terms_hbm.at[0:2, :, lanes], terms_ref.at[:, :, lanes], semaphores.at[at])

    @pl.when(step == 0)
    def _():
        thirds = [
            pltpu.make_async_copy(
                project_hbm.at[:, k * width : (k + 1) * width], project_ref.at[k], weight_semaphores.at[k]
            )
            for k in range(3)
        ]
        merge = pltpu.make_async_copy(merge_hbm, merge_ref, weight_semaphores.at[3])
        for copy in (*thirds, merge, terms_copy(0), terms_copy(1)):
            copy.start()
        tiles = width // LANES
        own = gathered_ref.shape[1] // (KINDS * tiles + 1)

        def tile(index):
            return gathered_ref[:, index * own : (index + 1) * own, :].reshape(-1, LANES)

        blocks = [
            jnp.concatenate([tile(k * tiles + t) for t in range(tiles)], axis=1) for k in range(KINDS)
        ]
        rows = jnp.concatenate(blocks[:-1], axis=0)
        update = dot_nt(tile(KINDS * tiles), down_ref[...]).astype(BF16)
        thirds[0].wait()
        query_ref[...] = dot(blocks[-1], project_ref[0]).astype(BF16)
        thirds[1].wait()
        key_ref[...] = dot(rows, project_ref[1]).astype(BF16)
        thirds[2].wait()
        value_ref[...] = dot(rows, project_ref[2]).astype(BF16)
        merge.wait()
        mix_ref[...] = dot_nt(update, merge_ref[...]).astype(BF16)

    @pl.when(step < steps - 2)
    def _():
        terms_copy(step + 2).start()

    terms_copy(step).wait()
    mask = head_mask(heads, width, heads)

    def expanded(ref, at):
        own = pl.ds(pl.multiple_of(at * part_rows, part_rows), part_rows)
        spread_out = ref[own, :].astype(F32)[:, None, :] * mask[None]
        return spread_out.reshape(part_rows * heads, width).astype(BF16)

    values = value_ref[...]
    all_rounded = []
    for sub in range(ATTEND_STACK):
        at = step * ATTEND_STACK + sub
        inside = slice(sub * part_lanes, (sub + 1) * part_lanes)
        lanes = pl.ds(pl.multiple_of(at * part_lanes, part_lanes), part_lanes)
        bias = terms_ref[0, :, lanes]
        scores = dot_nt(key_ref[...], expanded(query_ref, at)) * (width // heads) ** -0.5 + bias
        grad_probs = dot_nt(values, expanded(mix_ref, at))
        row_max = jnp.max(scores, axis=0, keepdims=True).astype(BF16).astype(F32)
        weights = jnp.exp(scores - row_max)
        row_total = jnp.sum(weights, axis=0, keepdims=True)
        rounded = weights.astype(BF16)
        all_rounded.append(rounded)
        inner = jnp.sum(rounded.astype(F32) * grad_probs, axis=0, keepdims=True)
        weight_ref[:, inside] = (weights * terms_ref[1, :, lanes]).astype(BF16)
        grad_ref[:, inside] = grad_probs
        small_ref[:, inside] = bias.astype(BF16)
        for k, stat in enumerate((row_max, row_total, inner)):
            for p in range(part_lanes // LANES):
                row = k * stat_rows + at * (part_lanes // LANES) + p
                stat_ref[pl.ds(row, 1), :] = stat[:, p * LANES : (p + 1) * LANES]
    mixture = dot_tn(jnp.concatenate(all_rounded, axis=1), values).reshape(-1, heads, width) * mask[None]
    part = jnp.sum(mixture, axis=1).astype(BF16)
    for sub in range(ATTEND_STACK):
        for t in range(width // LANES):
            low = 5 * stat_rows + t * part_rows
            send_ref[step * ATTEND_STACK + sub, low : low + part_rows, :] = part[
                sub * part_rows : (sub + 1) * part_rows, t * LANES : (t + 1) * LANES
            ]

    @pl.when(step == steps - 1)
    def _():
        pieces = [stat_ref[:stat_rows, :].astype(BF16)]
        for k in (1, 2):
            pieces.extend(split(stat_ref[k * stat_rows : (k + 1) * stat_rows, :]))
        stats = jnp.concatenate(pieces, axis=0)
        for c in range(owners):
            send_ref[c, : 5 * stat_rows, :] = stats


def attend_stage(gathered, project, down, merge, terms, owners):
    _, keys, lanes = terms.shape
    width = project.shape[0]
    count = gathered.shape[0] * gathered.shape[1] // (KINDS * (width // LANES) + 1)
    rows = count // owners
    steps = owners // ATTEND_STACK
    chunk = lanes // steps
    stat_rows = lanes // LANES
    payload = jax.ShapeDtypeStruct((owners, 5 * stat_rows + rows * width // LANES, LANES), BF16)
    tile = pl.BlockSpec((keys, chunk), lambda g: (0, g))
    arrays = (gathered, down)
    return pl.pallas_call(
        attend_kernel,
        grid=(steps,),
        in_specs=[whole(a) for a in arrays] + [pl.BlockSpec(memory_space=pl.ANY)] * 3,
        out_specs=(tile, tile, tile, whole(payload)),
        out_shape=(
            jax.ShapeDtypeStruct((keys, lanes), BF16),
            jax.ShapeDtypeStruct((keys, lanes), F32),
            jax.ShapeDtypeStruct((keys, lanes), BF16),
            payload,
        ),
        scratch_shapes=[
            pltpu.VMEM((count, width), BF16),
            pltpu.VMEM((count, width), BF16),
            pltpu.VMEM((keys, width), BF16),
            pltpu.VMEM((keys, width), BF16),
            pltpu.VMEM((3 * stat_rows, LANES), F32),
            pltpu.VMEM((3, width, width), BF16),
            pltpu.VMEM((width, width), BF16),
            pltpu.VMEM((2, keys, lanes), F32),
            pltpu.SemaphoreType.DMA((4,)),
            pltpu.SemaphoreType.DMA((steps,)),
        ],
        compiler_params=pltpu.CompilerParams(vmem_limit_bytes=ATTEND_LIMIT * MIB),
        cost_estimate=pl.CostEstimate(flops=8000 * MIB, bytes_accessed=12 * MIB, transcendentals=0),
        name="attend_stage",
    )(*arrays, project, merge, terms)


def combined(received_ref, rows):
    parts = received_ref.shape[0]

    def stat(part, index):
        return received_ref[part, index * rows : (index + 1) * rows, :].astype(F32)

    maxima = [stat(s, 0) for s in range(parts)]
    top = maxima[0]
    for s in range(1, parts):
        top = jnp.maximum(top, maxima[s])
    scales = [jnp.exp(value - top) for value in maxima]
    total = jnp.zeros_like(top)
    inner = jnp.zeros_like(top)
    for s in range(parts):
        total = total + scales[s] * (stat(s, 1) + stat(s, 2))
        inner = inner + scales[s] * (stat(s, 3) + stat(s, 4))
    return top, scales, total, inner


def update_tokens(
    received_ref, state_ref, hidden_ref, counts_ref, merge_ref, down_ref, weight_ref, positions_ref, update_ref,
    scales, total,
):
    column = lax.axis_index("col")
    tokens, width = state_ref.shape
    heads = TOKEN_HEADS
    parts = received_ref.shape[0]
    stat_rows = (received_ref.shape[1] - tokens * width // LANES) // 5
    halves = tokens // GROUP
    sub = iota((tokens, LANES), 0)
    mine = iota((tokens, LANES), 1) // heads == sub % GROUP
    stat_row = iota((stat_rows, LANES), 0)
    rows = []
    for s in range(parts):
        scale = scales[s] / total
        picked = jnp.zeros((tokens, LANES), F32)
        for p in range(halves):
            one = jnp.sum(jnp.where(stat_row == column * halves + p, scale, 0.0), axis=0, keepdims=True)
            picked = jnp.where(sub // GROUP == p, one, picked)
        rows.append(jnp.where(mine, picked, 0.0))
    stacked = jnp.concatenate(rows, axis=0)
    spread_out = head_mask(LANES, width, heads).astype(BF16)
    high, low = split(stacked)
    rest = stacked - high.astype(F32) - low.astype(F32)
    scale = dot(high, spread_out) + dot(low, spread_out) + dot(rest.astype(BF16), spread_out)
    pieces = []
    for t in range(width // LANES):
        at = 5 * stat_rows + t * tokens
        piece = jnp.zeros((tokens, LANES), F32)
        for s in range(parts):
            factor = scale[s * tokens : (s + 1) * tokens, t * LANES : (t + 1) * LANES]
            piece = piece + factor * received_ref[s, at : at + tokens, :].astype(F32)
        pieces.append(piece.astype(BF16))
    attention = jnp.concatenate(pieces, axis=1)
    update = (state_ref[...] + dot(attention, merge_ref[...])).astype(BF16)
    update_ref[...] = update
    lowered = dot(update, down_ref[...]).astype(BF16)
    atoms = hidden_ref.shape[0]
    counts_row = counts_ref[...].astype(F32)
    square = jnp.broadcast_to(counts_row, (tokens, tokens))
    above = iota((tokens, tokens), 0)
    below = iota((tokens, tokens), 1)
    counts_col = jnp.sum(jnp.where(above == below, square, 0.0), axis=1, keepdims=True)
    ends = jnp.sum(jnp.where(below <= above, square, 0.0), axis=1, keepdims=True)
    atom = iota((tokens, atoms), 1).astype(F32)
    member = ((atom < ends) & (atom >= ends - counts_col)).astype(F32).astype(BF16)
    hidden_next = (hidden_ref[...].astype(F32) + dot_tn(member, lowered)).astype(BF16)
    positions_ref[...] = dot_nt(weight_ref[...], hidden_next)


def gradient_kernel(
    weight_ref, grad_ref, small_ref, standard_ref, received_ref, own_ref, gain_ref, bias_weight_ref,
    state_ref, hidden_ref, counts_ref, merge_ref, down_ref, position_ref,
    out_hbm, positions_ref, update_ref, block_ref, ones_ref, factor_ref, inner_ref, slots_ref, semaphores,
):
    step = pl.program_id(0)
    heads, width = bias_weight_ref.shape
    rows = factor_ref.shape[0]

    @pl.when(step == 0)
    def _():
        lane = iota((heads, LANES), 1)
        repeat = (lane % heads == iota((heads, LANES), 0)).astype(BF16)
        tiled = dot_tn(repeat, bias_weight_ref[...]) * gain_ref[...][None, :]
        tiled = tiled - jnp.mean(tiled, axis=1, keepdims=True)
        high, low = split(tiled)
        owner = iota((LANES, width), 0) // heads
        for i in range(GROUP):
            mine = owner == i
            at = slice(i * width, (i + 1) * width)
            block_ref[:LANES, at] = jnp.where(mine, high.astype(F32), 0.0).astype(BF16)
            block_ref[LANES:, at] = jnp.where(mine, low.astype(F32), 0.0).astype(BF16)
            ones = jnp.where(mine, 1.0 / width, 0.0).astype(BF16)
            ones_ref[:LANES, at] = ones
            ones_ref[LANES:, at] = ones
        top, _, total, inner = combined(received_ref, rows)
        factor_ref[...] = jnp.exp(own_ref[0, :rows, :].astype(F32) - top) / total
        inner_ref[...] = inner / total

    steps = pl.num_programs(0)
    slot = step % 2
    count = slots_ref.shape[1]

    def out_copy(at):
        return pltpu.make_async_copy(
            slots_ref.at[at % 2], out_hbm.at[pl.ds(at * count, count)], semaphores.at[at % 2]
        )

    @pl.when(step >= 2)
    def _():
        out_copy(step - 2).wait()

    keys = weight_ref.shape[0]
    lefts, rights = [], []
    for q in range(STACK):
        lanes = slice(q * LANES, (q + 1) * LANES)
        factor = factor_ref[pl.ds(step * STACK + q, 1), :]
        inner = inner_ref[pl.ds(step * STACK + q, 1), :]
        grad = weight_ref[:, lanes].astype(F32) * factor * (grad_ref[:, lanes] - inner)
        rounded = grad.astype(BF16)
        lefts.append(jnp.concatenate([rounded, rounded], axis=1))
        rights.append(jnp.concatenate(split(grad * small_ref[:, lanes].astype(F32)), axis=1))
    left = jnp.concatenate(lefts, axis=0)
    right = jnp.concatenate(rights, axis=0)
    for i in range(0, GROUP, 2):
        at = slice(i * width, (i + 2) * width)
        direct = dot(left, block_ref[:, at])
        along = dot(right, ones_ref[:, at])
        for q in range(STACK):
            for k in range(2):
                part = (slice(q * keys, (q + 1) * keys), slice(k * width, (k + 1) * width))
                r = q * GROUP + i + k
                slots_ref[slot, r] = (direct[part] - standard_ref[r].astype(F32) * along[part]).astype(BF16)

    out_copy(step).start()

    @pl.when(step == steps - 1)
    def _():
        _, scales, total, _ = combined(received_ref, rows)
        update_tokens(
            received_ref, state_ref, hidden_ref, counts_ref, merge_ref, down_ref, position_ref,
            positions_ref, update_ref, scales, total,
        )
        out_copy(step - 1).wait()
        out_copy(step).wait()


def gradient_stage(weights, grad, small, standard, received, own, gain, bias_weight, state, hidden, counts, merge, down, weight):
    rows, keys, width = standard.shape
    arrays = (received, own, gain, bias_weight, state, hidden, counts, merge, down, weight)
    outs = (
        jax.ShapeDtypeStruct((weight.shape[0], hidden.shape[0]), F32),
        jax.ShapeDtypeStruct(state.shape, BF16),
    )
    tile = pl.BlockSpec((keys, STACK * LANES), lambda g: (0, g))
    block = pl.BlockSpec((STACK * GROUP, keys, width), lambda g: (g, 0, 0))
    return pl.pallas_call(
        gradient_kernel,
        grid=(rows // GROUP // STACK,),
        in_specs=[tile, tile, tile, block] + [whole(a) for a in arrays],
        out_specs=(pl.BlockSpec(memory_space=pl.ANY), *(whole(a) for a in outs)),
        out_shape=(jax.ShapeDtypeStruct(standard.shape, BF16), *outs),
        scratch_shapes=[
            pltpu.VMEM((2 * LANES, GROUP * width), BF16),
            pltpu.VMEM((2 * LANES, GROUP * width), BF16),
            pltpu.VMEM((rows // GROUP, LANES), F32),
            pltpu.VMEM((rows // GROUP, LANES), F32),
            pltpu.VMEM((2, STACK * GROUP, keys, width), BF16),
            pltpu.SemaphoreType.DMA((2,)),
        ],
        compiler_params=pltpu.CompilerParams(vmem_limit_bytes=GRADIENT_LIMIT * MIB),
        cost_estimate=pl.CostEstimate(flops=16000 * MIB, bytes_accessed=22 * MIB, transcendentals=0),
        name="gradient_stage",
    )(weights, grad, small, standard, *arrays)


def per_device(
    atom_feats, atom_gain, atom_project, atom_merge, atom_up, token_counts, token_single, token_gain,
    token_project, token_merge, pair_state, pair_gain, bias_weight, atom_down, position_weight,
    position_cotangent,
):
    both = ("row", "col")
    rows, columns = lax.axis_size("row"), lax.axis_size("col")
    devices = rows * columns
    right = lax.ppermute(atom_feats, both, [(i + 1, i) for i in range(devices - 1)])
    left = lax.ppermute(atom_feats, both, [(i, i + 1) for i in range(devices - 1)])
    gain = pair_gain
    bias_turned = bias_weight.T
    groups = pair_state.shape[0] // GROUP
    cuts = (0, groups // 4, groups * 5 // 8, groups)
    pair_part = pair_forward(pair_state, gain, bias_turned, 0, cuts[1])
    hidden, state, packed, send = atom_stage(
        left, atom_feats, right, atom_gain, atom_project, atom_merge, atom_up,
        token_counts, token_single, token_gain, position_weight, position_cotangent, rows, pair_part[0],
    )
    pair_part = pair_forward(pair_state, gain, bias_turned, cuts[1], cuts[2] - cuts[1], pair_part, (send,))
    shared = lax.all_to_all(send, "row", 0, 0)
    shared = shared.reshape(columns, -1, shared.shape[-1])
    mixed = jnp.concatenate([shared, jnp.broadcast_to(packed[None], (columns,) + packed.shape)], axis=1)
    gathered = lax.all_to_all(mixed, "col", 0, 0)
    terms, standard = pair_forward(
        pair_state, gain, bias_turned, cuts[2], cuts[3] - cuts[2], pair_part, (mixed,)
    )
    weights, grad, small, payload = attend_stage(
        gathered, token_project, atom_down, token_merge, terms, columns
    )
    received = lax.all_to_all(payload, "col", 0, 0)
    pair_grad, positions, token_update = gradient_stage(
        weights, grad, small, standard, received, payload, gain, bias_turned,
        state, hidden, token_counts, token_merge, atom_down, position_weight,
    )
    return (positions, token_update, pair_grad)


def solution(mesh):
    placed = (
        P(("row", "col"), None), P(), P(), P(), P(), P(("row", "col"), None), P(("row", "col"), None), P(),
        P(), P(), P("row", "col", None), P(), P(), P(), P(), P(None, ("row", "col")),
    )
    return jax.shard_map(
        per_device,
        mesh=mesh,
        in_specs=placed,
        out_specs=(P(None, ("row", "col")), P(("row", "col"), None), P("row", "col", None)),
        check_vma=False,
    )
```

```python
import jax
import jax.numpy as jnp
from jax import lax
from jax.experimental import pallas as pl
from jax.experimental.pallas import tpu as pltpu
from jax.sharding import PartitionSpec as P

ATOM_HEADS = 4
TOKEN_HEADS = 16
EPS = 1e-05
NEGATIVE = -1e30
LEFT, RIGHT = 48, 80
WINDOW = 32
KEYS = 128
LANES = 128
GROUP = 8
TERM_SLOTS = 8
KINDS = 3
ATTEND_STACK = 4
PAIR_STACK = 2
STACK = 4
F32 = jnp.float32
BF16 = jnp.bfloat16
NT = (((1,), (1,)), ((), ()))
TN = (((0,), (0,)), ((), ()))
MIB = 1 << 20
PAIR_LIMIT = 56
ATOM_LIMIT = 40
ATTEND_LIMIT = 46
GRADIENT_LIMIT = 32


def iota(shape, axis):
    return lax.broadcasted_iota(jnp.int32, shape, axis)


def dot(a, b):
    return jnp.dot(a, b, preferred_element_type=F32)


def dot_nt(a, b):
    return lax.dot_general(a, b, NT, preferred_element_type=F32)


def dot_tn(a, b):
    return lax.dot_general(a, b, TN, preferred_element_type=F32)


def split(value):
    high = value.astype(BF16)
    return high, (value - high.astype(F32)).astype(BF16)


def normalize(values, gain):
    center = values - jnp.mean(values, axis=-1, keepdims=True)
    spread = lax.rsqrt(jnp.mean(center * center, axis=-1, keepdims=True) + EPS)
    return center * spread * gain


def head_mask(rows, width, heads):
    size = width // heads
    head = iota((rows, width), 0) % heads
    column = iota((rows, width), 1)
    return ((column >= head * size) & (column < (head + 1) * size)).astype(F32)


def pair_kernel(x_ref, gain_ref, weight_ref, *rest):
    terms_ref, standard_ref, block_ref, ones_ref, normed_ref = rest[-5:]
    heads = weight_ref.shape[0]
    width = x_ref.shape[2]

    @pl.when(pl.program_id(0) == 0)
    def _():
        lane = iota((heads, LANES), 1)
        repeat = (lane % heads == iota((heads, LANES), 0)).astype(BF16)
        tiled = dot_tn(weight_ref[...], repeat)
        owner = iota((width, LANES), 1) // heads
        for i in range(GROUP):
            block_ref[i * width : (i + 1) * width, :] = jnp.where(owner == i, tiled, 0.0).astype(BF16)
        ones_ref[...] = jnp.full((width, width), 1.0 / width, BF16)

    gain = gain_ref[...][None, :]
    keys = x_ref.shape[1]
    owner = iota((keys, LANES), 1) // heads
    for q in range(PAIR_STACK):
        lanes = slice(q * LANES, (q + 1) * LANES)
        spread_all = jnp.zeros((keys, LANES), F32)
        for i in range(GROUP):
            x = x_ref[q * GROUP + i]
            center = x.astype(F32) - dot(x, ones_ref[...])
            spread = lax.rsqrt(jnp.sum(center * center, axis=1, keepdims=True) * (1.0 / width) + EPS)
            standard = center * spread
            standard_ref[q * GROUP + i] = standard.astype(BF16)
            normed_ref[q * keys : (q + 1) * keys, i * width : (i + 1) * width] = (standard * gain).astype(BF16)
            spread_all = jnp.where(owner == i, spread, spread_all)
        terms_ref[1, :, lanes] = spread_all
    bias = dot(normed_ref[...], block_ref[...])
    for q in range(PAIR_STACK):
        terms_ref[0, :, q * LANES : (q + 1) * LANES] = bias[q * keys : (q + 1) * keys]


def pair_forward(pair, gain, weight, first, count, previous=(), after=()):
    rows, keys, width = pair.shape
    heads = weight.shape[0]
    lanes = rows * heads
    outs = (
        jax.ShapeDtypeStruct((TERM_SLOTS, keys, lanes), F32),
        jax.ShapeDtypeStruct(pair.shape, BF16),
    )
    before = tuple(previous)
    others = before + tuple(after)
    return pl.pallas_call(
        pair_kernel,
        grid=(count // PAIR_STACK,),
        in_specs=[
            pl.BlockSpec((PAIR_STACK * GROUP, keys, width), lambda g: (g + first // PAIR_STACK, 0, 0)),
            whole(gain),
            whole(weight),
        ]
        + [pl.BlockSpec(memory_space=pl.ANY)] * len(others),
        out_specs=(
            pl.BlockSpec((2, keys, PAIR_STACK * LANES), lambda g: (0, 0, g + first // PAIR_STACK)),
            pl.BlockSpec((PAIR_STACK * GROUP, keys, width), lambda g: (g + first // PAIR_STACK, 0, 0)),
        ),
        out_shape=outs,
        scratch_shapes=[
            pltpu.VMEM((GROUP * width, LANES), BF16),
            pltpu.VMEM((width, width), BF16),
            pltpu.VMEM((PAIR_STACK * keys, GROUP * width), BF16),
        ],
        input_output_aliases={3 + i: i for i in range(len(before))},
        compiler_params=pltpu.CompilerParams(vmem_limit_bytes=PAIR_LIMIT * MIB),
        cost_estimate=pl.CostEstimate(
            flops=count * GROUP * keys * width * 5000, bytes_accessed=count * GROUP * keys * width * 5, transcendentals=0
        ),
        name="pair_forward",
    )(pair, gain, weight, *others)


def atom_kernel(
    left_ref, own_ref, right_ref, gain_ref, project_ref, merge_ref, up_ref,
    counts_ref, single_ref, token_gain_ref, weight_ref, cotangent_ref, _,
    hidden_ref, state_ref, packed_ref, send_ref, key_ref, value_ref, query_ref, attended_ref,
):
    atoms, width = own_ref.shape
    tokens = single_ref.shape[0]
    rows, columns = lax.axis_size("row"), lax.axis_size("col")
    first = (lax.axis_index("row") * columns + lax.axis_index("col")) * atoms
    feats = jnp.concatenate(
        [left_ref[atoms - LEFT :, :], own_ref[...], right_ref[:RIGHT, :]], axis=0
    )
    normed = normalize(feats.astype(F32), gain_ref[...][None, :]).astype(BF16)
    projected = dot(normed, project_ref[...]).astype(BF16)
    query_ref[...] = projected[LEFT : LEFT + atoms, :width]
    key_ref[...] = projected[:, width : 2 * width]
    value_ref[...] = projected[:, 2 * width :]
    size = width // ATOM_HEADS
    stacked = ATOM_HEADS * WINDOW
    lane_head = iota((stacked, width), 1) // size
    row_head = iota((stacked, width), 0) // WINDOW
    mask = lane_head == row_head
    key_index = iota((stacked, KEYS), 1)
    total = rows * columns * atoms
    for b in range(atoms // WINDOW):
        at = b * WINDOW
        queries = jnp.concatenate([query_ref[at : at + WINDOW, :]] * ATOM_HEADS, axis=0)
        queries = jnp.where(mask, queries.astype(F32), 0.0).astype(BF16)
        scores = dot_nt(queries, key_ref[at : at + KEYS, :]) * size**-0.5
        position = first - LEFT + at + key_index
        scores = jnp.where((position >= 0) & (position < total), scores, NEGATIVE)
        weights = jnp.exp(scores - jnp.max(scores, axis=1, keepdims=True))
        row_total = jnp.sum(weights, axis=1, keepdims=True)
        mixture = dot(weights.astype(BF16), value_ref[at : at + KEYS, :]) / row_total
        mixture = jnp.where(mask, mixture, 0.0)
        joined = mixture[:WINDOW]
        for h in range(1, ATOM_HEADS):
            joined = joined + mixture[h * WINDOW : (h + 1) * WINDOW]
        attended_ref[at : at + WINDOW, :] = joined.astype(BF16)
    hidden = (own_ref[...].astype(F32) + dot(attended_ref[...], merge_ref[...])).astype(BF16)
    hidden_ref[...] = hidden
    lifted = jnp.maximum(dot(hidden, up_ref[...]), 0.0).astype(BF16)
    counts_row = counts_ref[...].astype(F32)
    square = jnp.broadcast_to(counts_row, (tokens, tokens))
    above = iota((tokens, tokens), 0)
    below = iota((tokens, tokens), 1)
    counts_col = jnp.sum(jnp.where(above == below, square, 0.0), axis=1, keepdims=True)
    ends = jnp.sum(jnp.where(below <= above, square, 0.0), axis=1, keepdims=True)
    atom = iota((tokens, atoms), 1).astype(F32)
    member = ((atom < ends) & (atom >= ends - counts_col)).astype(F32).astype(BF16)
    state = dot(member, lifted) / counts_col + single_ref[...].astype(F32)
    state_ref[...] = state
    token_normed = normalize(state, token_gain_ref[...][None, :]).astype(BF16)
    turned = jnp.transpose(
        jnp.concatenate([cotangent_ref[...], jnp.zeros((LANES - 3, atoms), F32)], axis=0)
    )
    position_weight = weight_ref[...].astype(F32)
    grad_hidden = turned[:, 0:1] * position_weight[0:1, :]
    for k in range(1, 3):
        grad_hidden = grad_hidden + turned[:, k : k + 1] * position_weight[k : k + 1, :]
    grad_tokens = dot(member, grad_hidden.astype(BF16)).astype(BF16)
    tiles = [token_normed[:, t * LANES : (t + 1) * LANES] for t in range(token_normed.shape[1] // LANES)]
    block = jnp.concatenate(tiles, axis=0)
    packed_ref[...] = jnp.concatenate([block, grad_tokens], axis=0)
    for c in range(send_ref.shape[0]):
        send_ref[c] = block


def whole(array):
    zeros = (0,) * array.ndim
    return pl.BlockSpec(array.shape, lambda *_: zeros)


def atom_stage(left, own, right, gain, project, merge, up, counts, single, token_gain, weight, cotangent, copies, after):
    atoms, width = own.shape
    tokens, token_width = single.shape
    arrays = (left, own, right, gain, project, merge, up, counts, single, token_gain, weight, cotangent)
    outs = (
        jax.ShapeDtypeStruct((atoms, width), BF16),
        jax.ShapeDtypeStruct((tokens, token_width), F32),
        jax.ShapeDtypeStruct((tokens * token_width // LANES + tokens, LANES), BF16),
        jax.ShapeDtypeStruct((copies, tokens * token_width // LANES, LANES), BF16),
    )
    return pl.pallas_call(
        atom_kernel,
        grid=(1,),
        in_specs=[whole(a) for a in arrays]
        + [pl.BlockSpec(memory_space=pl.ANY)],
        out_specs=tuple(whole(a) for a in outs),
        out_shape=outs,
        scratch_shapes=[
            pltpu.VMEM((LEFT + atoms + RIGHT, width), BF16),
            pltpu.VMEM((LEFT + atoms + RIGHT, width), BF16),
            pltpu.VMEM((atoms, width), BF16),
            pltpu.VMEM((atoms, width), BF16),
        ],
        compiler_params=pltpu.CompilerParams(vmem_limit_bytes=ATOM_LIMIT * MIB),
        cost_estimate=pl.CostEstimate(flops=400 * MIB, bytes_accessed=2 * MIB, transcendentals=0),
        name="atom_stage",
    )(*arrays, after)


def attend_kernel(
    gathered_ref, down_ref, project_hbm, merge_hbm, terms_hbm,
    weight_ref, grad_ref, small_ref, send_ref,
    query_ref, mix_ref, key_ref, value_ref, stat_ref, project_ref, merge_ref, terms_ref,
    weight_semaphores, semaphores,
):
    step = pl.program_id(0)
    owners = send_ref.shape[0]
    steps = owners // ATTEND_STACK
    width = project_ref.shape[1]
    heads = TOKEN_HEADS
    chunk = weight_ref.shape[1]
    per = chunk // LANES
    stat_rows = steps * per
    part_rows = query_ref.shape[0] // owners
    part_lanes = chunk // ATTEND_STACK

    def terms_copy(at):
        lanes = pl.ds(pl.multiple_of(at * chunk, chunk), chunk)
        return pltpu.make_async_copy(terms_hbm.at[0:2, :, lanes], terms_ref.at[:, :, lanes], semaphores.at[at])

    @pl.when(step == 0)
    def _():
        thirds = [
            pltpu.make_async_copy(
                project_hbm.at[:, k * width : (k + 1) * width], project_ref.at[k], weight_semaphores.at[k]
            )
            for k in range(3)
        ]
        merge = pltpu.make_async_copy(merge_hbm, merge_ref, weight_semaphores.at[3])
        for copy in (*thirds, merge, terms_copy(0), terms_copy(1)):
            copy.start()
        tiles = width // LANES
        own = gathered_ref.shape[1] // (KINDS * tiles + 1)

        def tile(index):
            return gathered_ref[:, index * own : (index + 1) * own, :].reshape(-1, LANES)

        blocks = [
            jnp.concatenate([tile(k * tiles + t) for t in range(tiles)], axis=1) for k in range(KINDS)
        ]
        rows = jnp.concatenate(blocks[:-1], axis=0)
        update = dot_nt(tile(KINDS * tiles), down_ref[...]).astype(BF16)
        thirds[0].wait()
        query_ref[...] = dot(blocks[-1], project_ref[0]).astype(BF16)
        thirds[1].wait()
        key_ref[...] = dot(rows, project_ref[1]).astype(BF16)
        thirds[2].wait()
        value_ref[...] = dot(rows, project_ref[2]).astype(BF16)
        merge.wait()
        mix_ref[...] = dot_nt(update, merge_ref[...]).astype(BF16)

    @pl.when(step < steps - 2)
    def _():
        terms_copy(step + 2).start()

    terms_copy(step).wait()
    mask = head_mask(heads, width, heads)

    def expanded(ref, at):
        own = pl.ds(pl.multiple_of(at * part_rows, part_rows), part_rows)
        spread_out = ref[own, :].astype(F32)[:, None, :] * mask[None]
        return spread_out.reshape(part_rows * heads, width).astype(BF16)

    values = value_ref[...]
    all_rounded = []
    for sub in range(ATTEND_STACK):
        at = step * ATTEND_STACK + sub
        inside = slice(sub * part_lanes, (sub + 1) * part_lanes)
        lanes = pl.ds(pl.multiple_of(at * part_lanes, part_lanes), part_lanes)
        bias = terms_ref[0, :, lanes]
        scores = dot_nt(key_ref[...], expanded(query_ref, at)) * (width // heads) ** -0.5 + bias
        grad_probs = dot_nt(values, expanded(mix_ref, at))
        row_max = jnp.max(scores, axis=0, keepdims=True).astype(BF16).astype(F32)
        weights = jnp.exp(scores - row_max)
        row_total = jnp.sum(weights, axis=0, keepdims=True)
        rounded = weights.astype(BF16)
        all_rounded.append(rounded)
        inner = jnp.sum(rounded.astype(F32) * grad_probs, axis=0, keepdims=True)
        weight_ref[:, inside] = (weights * terms_ref[1, :, lanes]).astype(BF16)
        grad_ref[:, inside] = grad_probs
        small_ref[:, inside] = bias.astype(BF16)
        for k, stat in enumerate((row_max, row_total, inner)):
            for p in range(part_lanes // LANES):
                row = k * stat_rows + at * (part_lanes // LANES) + p
                stat_ref[pl.ds(row, 1), :] = stat[:, p * LANES : (p + 1) * LANES]
    mixture = dot_tn(jnp.concatenate(all_rounded, axis=1), values).reshape(-1, heads, width) * mask[None]
    part = jnp.sum(mixture, axis=1).astype(BF16)
    for sub in range(ATTEND_STACK):
        for t in range(width // LANES):
            low = 5 * stat_rows + t * part_rows
            send_ref[step * ATTEND_STACK + sub, low : low + part_rows, :] = part[
                sub * part_rows : (sub + 1) * part_rows, t * LANES : (t + 1) * LANES
            ]

    @pl.when(step == steps - 1)
    def _():
        pieces = [stat_ref[:stat_rows, :].astype(BF16)]
        for k in (1, 2):
            pieces.extend(split(stat_ref[k * stat_rows : (k + 1) * stat_rows, :]))
        stats = jnp.concatenate(pieces, axis=0)
        for c in range(owners):
            send_ref[c, : 5 * stat_rows, :] = stats


def attend_stage(gathered, project, down, merge, terms, owners):
    _, keys, lanes = terms.shape
    width = project.shape[0]
    count = gathered.shape[0] * gathered.shape[1] // (KINDS * (width // LANES) + 1)
    rows = count // owners
    steps = owners // ATTEND_STACK
    chunk = lanes // steps
    stat_rows = lanes // LANES
    payload = jax.ShapeDtypeStruct((owners, 5 * stat_rows + rows * width // LANES, LANES), BF16)
    tile = pl.BlockSpec((keys, chunk), lambda g: (0, g))
    arrays = (gathered, down)
    return pl.pallas_call(
        attend_kernel,
        grid=(steps,),
        in_specs=[whole(a) for a in arrays] + [pl.BlockSpec(memory_space=pl.ANY)] * 3,
        out_specs=(tile, tile, tile, whole(payload)),
        out_shape=(
            jax.ShapeDtypeStruct((keys, lanes), BF16),
            jax.ShapeDtypeStruct((keys, lanes), F32),
            jax.ShapeDtypeStruct((keys, lanes), BF16),
            payload,
        ),
        scratch_shapes=[
            pltpu.VMEM((count, width), BF16),
            pltpu.VMEM((count, width), BF16),
            pltpu.VMEM((keys, width), BF16),
            pltpu.VMEM((keys, width), BF16),
            pltpu.VMEM((3 * stat_rows, LANES), F32),
            pltpu.VMEM((3, width, width), BF16),
            pltpu.VMEM((width, width), BF16),
            pltpu.VMEM((2, keys, lanes), F32),
            pltpu.SemaphoreType.DMA((4,)),
            pltpu.SemaphoreType.DMA((steps,)),
        ],
        compiler_params=pltpu.CompilerParams(vmem_limit_bytes=ATTEND_LIMIT * MIB),
        cost_estimate=pl.CostEstimate(flops=8000 * MIB, bytes_accessed=12 * MIB, transcendentals=0),
        name="attend_stage",
    )(*arrays, project, merge, terms)


def combined(received_ref, rows):
    parts = received_ref.shape[0]

    def stat(part, index):
        return received_ref[part, index * rows : (index + 1) * rows, :].astype(F32)

    maxima = [stat(s, 0) for s in range(parts)]
    top = maxima[0]
    for s in range(1, parts):
        top = jnp.maximum(top, maxima[s])
    scales = [jnp.exp(value - top) for value in maxima]
    total = jnp.zeros_like(top)
    inner = jnp.zeros_like(top)
    for s in range(parts):
        total = total + scales[s] * (stat(s, 1) + stat(s, 2))
        inner = inner + scales[s] * (stat(s, 3) + stat(s, 4))
    return top, scales, total, inner


def update_tokens(
    received_ref, state_ref, hidden_ref, counts_ref, merge_ref, down_ref, weight_ref, positions_ref, update_ref,
    scales, total,
):
    column = lax.axis_index("col")
    tokens, width = state_ref.shape
    heads = TOKEN_HEADS
    parts = received_ref.shape[0]
    stat_rows = (received_ref.shape[1] - tokens * width // LANES) // 5
    halves = tokens // GROUP
    sub = iota((tokens, LANES), 0)
    mine = iota((tokens, LANES), 1) // heads == sub % GROUP
    stat_row = iota((stat_rows, LANES), 0)
    rows = []
    for s in range(parts):
        scale = scales[s] / total
        picked = jnp.zeros((tokens, LANES), F32)
        for p in range(halves):
            one = jnp.sum(jnp.where(stat_row == column * halves + p, scale, 0.0), axis=0, keepdims=True)
            picked = jnp.where(sub // GROUP == p, one, picked)
        rows.append(jnp.where(mine, picked, 0.0))
    stacked = jnp.concatenate(rows, axis=0)
    spread_out = head_mask(LANES, width, heads).astype(BF16)
    high, low = split(stacked)
    rest = stacked - high.astype(F32) - low.astype(F32)
    scale = dot(high, spread_out) + dot(low, spread_out) + dot(rest.astype(BF16), spread_out)
    pieces = []
    for t in range(width // LANES):
        at = 5 * stat_rows + t * tokens
        piece = jnp.zeros((tokens, LANES), F32)
        for s in range(parts):
            factor = scale[s * tokens : (s + 1) * tokens, t * LANES : (t + 1) * LANES]
            piece = piece + factor * received_ref[s, at : at + tokens, :].astype(F32)
        pieces.append(piece.astype(BF16))
    attention = jnp.concatenate(pieces, axis=1)
    update = (state_ref[...] + dot(attention, merge_ref[...])).astype(BF16)
    update_ref[...] = update
    lowered = dot(update, down_ref[...]).astype(BF16)
    atoms = hidden_ref.shape[0]
    counts_row = counts_ref[...].astype(F32)
    square = jnp.broadcast_to(counts_row, (tokens, tokens))
    above = iota((tokens, tokens), 0)
    below = iota((tokens, tokens), 1)
    counts_col = jnp.sum(jnp.where(above == below, square, 0.0), axis=1, keepdims=True)
    ends = jnp.sum(jnp.where(below <= above, square, 0.0), axis=1, keepdims=True)
    atom = iota((tokens, atoms), 1).astype(F32)
    member = ((atom < ends) & (atom >= ends - counts_col)).astype(F32).astype(BF16)
    hidden_next = (hidden_ref[...].astype(F32) + dot_tn(member, lowered)).astype(BF16)
    positions_ref[...] = dot_nt(weight_ref[...], hidden_next)


def gradient_kernel(
    weight_ref, grad_ref, small_ref, standard_ref, received_ref, own_ref, gain_ref, bias_weight_ref,
    state_ref, hidden_ref, counts_ref, merge_ref, down_ref, position_ref,
    out_hbm, positions_ref, update_ref, block_ref, ones_ref, factor_ref, inner_ref, slots_ref, semaphores,
):
    step = pl.program_id(0)
    heads, width = bias_weight_ref.shape
    rows = factor_ref.shape[0]

    @pl.when(step == 0)
    def _():
        lane = iota((heads, LANES), 1)
        repeat = (lane % heads == iota((heads, LANES), 0)).astype(BF16)
        tiled = dot_tn(repeat, bias_weight_ref[...]) * gain_ref[...][None, :]
        tiled = tiled - jnp.mean(tiled, axis=1, keepdims=True)
        high, low = split(tiled)
        owner = iota((LANES, width), 0) // heads
        for i in range(GROUP):
            mine = owner == i
            at = slice(i * width, (i + 1) * width)
            block_ref[:LANES, at] = jnp.where(mine, high.astype(F32), 0.0).astype(BF16)
            block_ref[LANES:, at] = jnp.where(mine, low.astype(F32), 0.0).astype(BF16)
            ones = jnp.where(mine, 1.0 / width, 0.0).astype(BF16)
            ones_ref[:LANES, at] = ones
            ones_ref[LANES:, at] = ones
        top, _, total, inner = combined(received_ref, rows)
        factor_ref[...] = jnp.exp(own_ref[0, :rows, :].astype(F32) - top) / total
        inner_ref[...] = inner / total

    steps = pl.num_programs(0)
    slot = step % 2
    count = slots_ref.shape[1]

    def out_copy(at):
        return pltpu.make_async_copy(
            slots_ref.at[at % 2], out_hbm.at[pl.ds(at * count, count)], semaphores.at[at % 2]
        )

    @pl.when(step >= 2)
    def _():
        out_copy(step - 2).wait()

    keys = weight_ref.shape[0]
    lefts, rights = [], []
    for q in range(STACK):
        lanes = slice(q * LANES, (q + 1) * LANES)
        factor = factor_ref[pl.ds(step * STACK + q, 1), :]
        inner = inner_ref[pl.ds(step * STACK + q, 1), :]
        grad = weight_ref[:, lanes].astype(F32) * factor * (grad_ref[:, lanes] - inner)
        rounded = grad.astype(BF16)
        lefts.append(jnp.concatenate([rounded, rounded], axis=1))
        rights.append(jnp.concatenate(split(grad * small_ref[:, lanes].astype(F32)), axis=1))
    left = jnp.concatenate(lefts, axis=0)
    right = jnp.concatenate(rights, axis=0)
    for i in range(0, GROUP, 2):
        at = slice(i * width, (i + 2) * width)
        direct = dot(left, block_ref[:, at])
        along = dot(right, ones_ref[:, at])
        for q in range(STACK):
            for k in range(2):
                part = (slice(q * keys, (q + 1) * keys), slice(k * width, (k + 1) * width))
                r = q * GROUP + i + k
                slots_ref[slot, r] = (direct[part] - standard_ref[r].astype(F32) * along[part]).astype(BF16)

    out_copy(step).start()

    @pl.when(step == steps - 1)
    def _():
        _, scales, total, _ = combined(received_ref, rows)
        update_tokens(
            received_ref, state_ref, hidden_ref, counts_ref, merge_ref, down_ref, position_ref,
            positions_ref, update_ref, scales, total,
        )
        out_copy(step - 1).wait()
        out_copy(step).wait()


def gradient_stage(weights, grad, small, standard, received, own, gain, bias_weight, state, hidden, counts, merge, down, weight):
    rows, keys, width = standard.shape
    arrays = (received, own, gain, bias_weight, state, hidden, counts, merge, down, weight)
    outs = (
        jax.ShapeDtypeStruct((weight.shape[0], hidden.shape[0]), F32),
        jax.ShapeDtypeStruct(state.shape, BF16),
    )
    tile = pl.BlockSpec((keys, STACK * LANES), lambda g: (0, g))
    block = pl.BlockSpec((STACK * GROUP, keys, width), lambda g: (g, 0, 0))
    return pl.pallas_call(
        gradient_kernel,
        grid=(rows // GROUP // STACK,),
        in_specs=[tile, tile, tile, block] + [whole(a) for a in arrays],
        out_specs=(pl.BlockSpec(memory_space=pl.ANY), *(whole(a) for a in outs)),
        out_shape=(jax.ShapeDtypeStruct(standard.shape, BF16), *outs),
        scratch_shapes=[
            pltpu.VMEM((2 * LANES, GROUP * width), BF16),
            pltpu.VMEM((2 * LANES, GROUP * width), BF16),
            pltpu.VMEM((rows // GROUP, LANES), F32),
            pltpu.VMEM((rows // GROUP, LANES), F32),
            pltpu.VMEM((2, STACK * GROUP, keys, width), BF16),
            pltpu.SemaphoreType.DMA((2,)),
        ],
        compiler_params=pltpu.CompilerParams(vmem_limit_bytes=GRADIENT_LIMIT * MIB),
        cost_estimate=pl.CostEstimate(flops=16000 * MIB, bytes_accessed=22 * MIB, transcendentals=0),
        name="gradient_stage",
    )(weights, grad, small, standard, *arrays)


def per_device(
    atom_feats, atom_gain, atom_project, atom_merge, atom_up, token_counts, token_single, token_gain,
    token_project, token_merge, pair_state, pair_gain, bias_weight, atom_down, position_weight,
    position_cotangent,
):
    both = ("row", "col")
    rows, columns = lax.axis_size("row"), lax.axis_size("col")
    devices = rows * columns
    right = lax.ppermute(atom_feats, both, [(i + 1, i) for i in range(devices - 1)])
    left = lax.ppermute(atom_feats, both, [(i, i + 1) for i in range(devices - 1)])
    gain = pair_gain
    bias_turned = bias_weight.T
    groups = pair_state.shape[0] // GROUP
    cuts = (0, groups // 4, groups // 2, groups)
    pair_part = pair_forward(pair_state, gain, bias_turned, 0, cuts[1])
    hidden, state, packed, send = atom_stage(
        left, atom_feats, right, atom_gain, atom_project, atom_merge, atom_up,
        token_counts, token_single, token_gain, position_weight, position_cotangent, rows, pair_part[0],
    )
    pair_part = pair_forward(pair_state, gain, bias_turned, cuts[1], cuts[2] - cuts[1], pair_part, (send,))
    shared = lax.all_to_all(send, "row", 0, 0)
    shared = shared.reshape(columns, -1, shared.shape[-1])
    mixed = jnp.concatenate([shared, jnp.broadcast_to(packed[None], (columns,) + packed.shape)], axis=1)
    gathered = lax.all_to_all(mixed, "col", 0, 0)
    terms, standard = pair_forward(
        pair_state, gain, bias_turned, cuts[2], cuts[3] - cuts[2], pair_part, (mixed,)
    )
    weights, grad, small, payload = attend_stage(
        gathered, token_project, atom_down, token_merge, terms, columns
    )
    received = lax.all_to_all(payload, "col", 0, 0)
    pair_grad, positions, token_update = gradient_stage(
        weights, grad, small, standard, received, payload, gain, bias_turned,
        state, hidden, token_counts, token_merge, atom_down, position_weight,
    )
    return (positions, token_update, pair_grad)


def solution(mesh):
    placed = (
        P(("row", "col"), None), P(), P(), P(), P(), P(("row", "col"), None), P(("row", "col"), None), P(),
        P(), P(), P("row", "col", None), P(), P(), P(), P(), P(None, ("row", "col")),
    )
    return jax.shard_map(
        per_device,
        mesh=mesh,
        in_specs=placed,
        out_specs=(P(None, ("row", "col")), P(("row", "col"), None), P("row", "col", None)),
        check_vma=False,
    )
```
